512 devices in a mesh: row: 16 (over z_lo, core), col: 32 (over y, z_hi, x).
Axes of the slice: x: 4, y: 4, z: 16 (z_hi: 2, z_lo: 8; z = z_hi * 8 + z_lo), core: 2. Of those that a mesh axis runs over, the one named last changes fastest.
Arguments:
- features: bfloat16 [65536, 512], P(('row', 'col')), may hold values from -6 to 6
- weight: bfloat16 [512, 512], replicated, may hold values from -0.25 to 0.25
- cotangent: bfloat16 [65536, 512], P(('row', 'col')), may hold values from -6 to 6
- tile_rows: int32 [16, 32, 8], P('row', 'col'), may hold values from 0 to 31
- tile_cols: int32 [16, 32, 8], P('row', 'col'), may hold values from 0 to 15
- tile_count: int32 [16, 32], P('row', 'col'), may hold values from 2 to 8, as said below
- tile_vals: bfloat16 [16, 32, 8, 128, 128], P('row', 'col'), may hold values from 0 to 3
Outputs:
- output: bfloat16 [65536, 512], P(('row', 'col'))
- weight_grad: float32 [512, 512], replicated
- feature_grad: float32 [65536, 512], P(('row', 'col'))
The draws below stay inside these ranges and needn't reach their ends.
Inputs may be any that keep to these rules, and one draw needn't show every extreme that they name: `tile_count`: some device has exactly 8 live slots; slots at or past the count are to be ignored. `tile_rows`: block rows of the tiles; tiles may repeat a position. `tile_cols`: block columns of the tiles.
All inputs are finite; a program needn't handle non-finite values.
Results may differ from the reference program's by a relative error of at most 0.015.
Values may be sent and summed in bfloat16 or wider, within the bound.
No kernel may reach another device: no remote copies, remote signals or barrier semaphores. Data moves between devices by JAX's collectives and lax.ppermute only.
A program may use at most 64 MiB of HBM per device.

```python
import math
import jax
import jax.numpy as jnp
from jax import lax

F = 512
BLK = 128
CH = 128
TILE_CAP = 8
NODES = 65536
N_ROW = 16
N_COL = 32


def draw_tile_count(key, part):
    key = jax.random.fold_in(key, 5)
    first_key, second_key = jax.random.split(key)
    counts = jax.random.randint(first_key, (N_ROW * N_COL,), TILE_CAP // 4, TILE_CAP + 1, dtype=jnp.int32)
    fullest = jax.random.randint(second_key, (), 0, N_ROW * N_COL, dtype=jnp.int32)
    counts = counts.at[fullest].set(TILE_CAP)
    return counts.reshape(N_ROW, N_COL).astype(jnp.int32)


def draw_tile_vals(key, part):
    key = jax.random.fold_in(key, 7)
    levels = jax.random.randint(key, (N_ROW, N_COL, TILE_CAP, BLK, BLK), 0, 4, dtype=jnp.int32)
    return levels.astype(jnp.float32).astype(jnp.bfloat16)


def with_ends(array, own_key, smallest, top_value):
    longest = array.shape.index(max(array.shape))
    spots = []
    for shift in (0, 1):
        where = [jax.random.randint(jax.random.fold_in(own_key, axis), (), 0, length) for axis, length in enumerate(array.shape)]
        where[longest] = (where[longest] + shift) % array.shape[longest]
        spots.append(tuple(where))
    return array.at[spots[0]].set(smallest).at[spots[1]].set(top_value)


def block_levels(own_key, dims, cuts, least, top_value):
    factor_of, own = 1.0, jax.random.fold_in(own_key, 6)
    for dim, shards_of in cuts:
        heights = jnp.exp(jax.random.uniform(jax.random.fold_in(own, dim), (shards_of,), jnp.float32, least / len(cuts), top_value / len(cuts)))
        factor_of = factor_of * jnp.repeat(heights, dims[dim] // shards_of).reshape([-1 if axis == dim else 1 for axis in range(len(dims))])
    return factor_of


def centred(key, extent, width, bound, cuts=(), kind=jnp.bfloat16):
    factor_of = block_levels(key, extent, cuts, -0.22, 0.18) if cuts else 1.0
    entries = jax.random.normal(key, extent, jnp.float32) * width * factor_of
    return jnp.minimum(jnp.maximum(entries, -bound), bound).astype(kind)


def setup_inputs(seed: int = 0) -> dict:
    arg_keys = jax.random.split(jax.random.key(seed), 8)
    features = centred(arg_keys[0], (NODES, F), 1.0, 6.0, ((0, 512),))
    weight = centred(arg_keys[1], (F, F), F ** -0.5, 0.25)
    cotangent = centred(arg_keys[2], (NODES, F), 1.0, 6.0, ((0, 512),))
    tile_rows = with_ends(jax.random.randint(arg_keys[3], (N_ROW, N_COL, TILE_CAP), 0, N_COL * CH // BLK), jax.random.fold_in(arg_keys[3], 1), 0, (N_COL * CH // BLK) - 1).astype(jnp.int32)
    tile_cols = with_ends(jax.random.randint(arg_keys[4], (N_ROW, N_COL, TILE_CAP), 0, N_ROW * CH // BLK), jax.random.fold_in(arg_keys[4], 1), 0, (N_ROW * CH // BLK) - 1).astype(jnp.int32)
    tile_count = draw_tile_count(jax.random.fold_in(arg_keys[7], 71), 0)
    tile_vals = draw_tile_vals(jax.random.fold_in(arg_keys[7], 71), 0)
    return {"features": features, "weight": weight, "cotangent": cotangent, "tile_rows": tile_rows, "tile_cols": tile_cols, "tile_count": tile_count, "tile_vals": tile_vals}


def live_weights(tile_block, slot_total):
    alive = (jnp.arange(TILE_CAP, dtype=jnp.int32) < slot_total).astype(jnp.float32)
    return tile_block.astype(jnp.float32) * alive[:, None, None]

def degree_part(tile_block, col_index, slot_total):
    weights = live_weights(tile_block, slot_total)
    col_sums = lax.optimization_barrier(jnp.sum(weights, axis=1))
    place_cols = (col_index[:, None] == jnp.arange(N_ROW * CH // BLK, dtype=jnp.int32)[None, :]).astype(jnp.float32)
    summed = jnp.einsum('sc,sj->cj', place_cols, col_sums, precision=lax.Precision.HIGHEST)
    return summed.reshape(N_ROW * CH)

def forward_part(tile_block, row_index, col_index, slot_total, source):
    weights = live_weights(tile_block, slot_total)
    picked = source.reshape(N_ROW * CH // BLK, BLK, F)[col_index].astype(jnp.float32)
    products = jnp.einsum('sij,sjf->sif', weights, picked, precision=lax.Precision.HIGHEST)
    place_rows = (row_index[:, None] == jnp.arange(N_COL * CH // BLK, dtype=jnp.int32)[None, :]).astype(jnp.float32)
    summed = jnp.einsum('sr,sif->rif', place_rows, products, precision=lax.Precision.HIGHEST)
    return summed.reshape(N_COL * CH, F)

def backward_part(tile_block, row_index, col_index, slot_total, source):
    weights = live_weights(tile_block, slot_total)
    picked = source.reshape(N_COL * CH // BLK, BLK, F)[row_index].astype(jnp.float32)
    products = jnp.einsum('sij,sif->sjf', weights, picked, precision=lax.Precision.HIGHEST)
    place_cols = (col_index[:, None] == jnp.arange(N_ROW * CH // BLK, dtype=jnp.int32)[None, :]).astype(jnp.float32)
    summed = jnp.einsum('sc,sjf->cjf', place_cols, products, precision=lax.Precision.HIGHEST)
    return summed.reshape(N_ROW * CH, F)

def reference(features, weight, cotangent, tile_rows, tile_cols, tile_count, tile_vals):
    row_ids = jnp.arange(N_ROW, dtype=jnp.int32)
    col_ids = jnp.arange(N_COL, dtype=jnp.int32)

    def degree_row(row_id):
        return jax.vmap(degree_part)(tile_vals[row_id], tile_cols[row_id], tile_count[row_id])
    col_degree = 1.0 + lax.optimization_barrier(jnp.sum(lax.map(degree_row, row_ids), axis=0))
    col_scale = lax.rsqrt(col_degree)
    col_groups = features.reshape(N_ROW, N_COL, CH, F).transpose(1, 0, 2, 3).reshape(N_COL, N_ROW * CH, F)
    scaled = (col_groups.astype(jnp.float32) * col_scale[:, :, None]).astype(jnp.bfloat16)

    def row_sum(row_id):

        def add_col(accum, col_id):
            part = forward_part(tile_vals[row_id, col_id], tile_rows[row_id, col_id], tile_cols[row_id, col_id], tile_count[row_id, col_id], scaled[col_id])
            rounded = lax.optimization_barrier(part.astype(jnp.bfloat16))
            return (accum + rounded.astype(jnp.float32), None)
        accum, unused = lax.scan(add_col, jnp.zeros((N_COL * CH, F), jnp.float32), col_ids)
        return accum
    row_total = lax.map(row_sum, row_ids).reshape(NODES, F)
    inv_rms = lax.rsqrt(lax.optimization_barrier(jnp.mean(row_total * row_total, axis=1, keepdims=True)) + 1e-06)
    norm_f32 = row_total * inv_rms
    normed = norm_f32.astype(jnp.bfloat16)
    pre_act = jnp.dot(normed, weight, preferred_element_type=jnp.float32)
    output = jax.nn.silu(pre_act).astype(jnp.bfloat16)
    sigmoid_pre = jax.nn.sigmoid(pre_act)
    act_slope = sigmoid_pre * (1.0 + pre_act * (1.0 - sigmoid_pre))
    grad_pre = (cotangent.astype(jnp.float32) * act_slope).astype(jnp.bfloat16)
    weight_grad = jnp.dot(normed.T, grad_pre, preferred_element_type=jnp.float32) * (1.0 / math.sqrt(NODES))
    grad_norm = jnp.dot(grad_pre, weight.T, preferred_element_type=jnp.float32)
    grad_z = (inv_rms * (grad_norm - norm_f32 * lax.optimization_barrier(jnp.mean(grad_norm * norm_f32, axis=1, keepdims=True)))).astype(jnp.bfloat16)
    grad_groups = grad_z.reshape(N_ROW, N_COL * CH, F)

    def col_sum(col_id):

        def add_row(accum, row_id):
            part = backward_part(tile_vals[row_id, col_id], tile_rows[row_id, col_id], tile_cols[row_id, col_id], tile_count[row_id, col_id], grad_groups[row_id])
            rounded = lax.optimization_barrier(part.astype(jnp.bfloat16))
            return (accum + rounded.astype(jnp.float32), None)
        accum, unused = lax.scan(add_row, jnp.zeros((N_ROW * CH, F), jnp.float32), row_ids)
        return accum
    col_total = lax.map(col_sum, col_ids)
    grad_cols = col_total * col_scale[:, :, None]
    feature_grad = grad_cols.reshape(N_COL, N_ROW, CH, F).transpose(1, 0, 2, 3).reshape(NODES, F)
    return (output, weight_grad, feature_grad)
```

```python
import math

import jax
import jax.numpy as jnp
from jax import lax
from jax.sharding import Mesh
from jax.sharding import PartitionSpec as P

AXES = ("zl", "core", "y", "zh", "x")
ROW = ("zl", "core")
PLANE = ("y", "x")
DEPTH = ("zl", "core", "zh")
BF16 = jnp.bfloat16
F32 = jnp.float32


def layer_rows(row_total, grad_rows, weight):
    inv_rms = lax.rsqrt(jnp.mean(row_total * row_total, axis=1, keepdims=True) + 1e-06)
    norm_f32 = row_total * inv_rms
    normed = norm_f32.astype(BF16)
    pre_act = jnp.dot(normed, weight, preferred_element_type=F32)
    output = jax.nn.silu(pre_act).astype(BF16)
    sigmoid_pre = jax.nn.sigmoid(pre_act)
    act_slope = sigmoid_pre * (1.0 + pre_act * (1.0 - sigmoid_pre))
    grad_pre = (grad_rows.astype(F32) * act_slope).astype(BF16)
    grad_norm = jnp.einsum("ng,fg->nf", grad_pre, weight, preferred_element_type=F32)
    grad_z = (
        inv_rms * (grad_norm - norm_f32 * jnp.mean(grad_norm * norm_f32, axis=1, keepdims=True))
    ).astype(BF16)
    return (output, normed, grad_pre, grad_z)


def exchange(block, axis):
    return lax.ppermute(block, axis, [(0, 1), (1, 0)])


def scatter_parts(parts, axes):
    return lax.all_to_all(parts, axes, split_axis=0, concat_axis=0, tiled=True)


def gather_copies(block, axes):
    count = lax.axis_size(axes)
    copies = jnp.broadcast_to(block[None], (count,) + block.shape)
    return lax.all_to_all(copies, axes, split_axis=0, concat_axis=0, tiled=True)


def local(features, weight, cotangent, tile_rows, tile_cols, tile_count, tile_vals):
    span, width = features.shape
    n_zl, n_core = lax.axis_size("zl"), lax.axis_size("core")
    n_y, n_zh, n_x = lax.axis_size("y"), lax.axis_size("zh"), lax.axis_size("x")
    n_row, n_col = n_zl * n_core, n_y * n_zh * n_x
    n_plane = n_y * n_x
    my_zl, my_core, my_zh = lax.axis_index("zl"), lax.axis_index("core"), lax.axis_index("zh")
    slots = tile_vals.shape[2]
    nodes = n_row * n_col * span
    alive = jnp.arange(slots, dtype=jnp.int32) < tile_count[0, 0]
    weights = tile_vals[0, 0] * alive.astype(BF16)[:, None, None]
    row_index = tile_rows[0, 0]
    col_index = tile_cols[0, 0]
    col_place = ((col_index % n_core) ^ my_core) * n_zl + col_index // n_core
    row_plane = (row_index // (n_zh * n_x)) * n_x + row_index % n_x
    row_place = (((row_index // n_x) % n_zh) ^ my_zh) * n_plane + row_plane
    place_rows = (row_place[:, None] == jnp.arange(n_col, dtype=jnp.int32)[None, :]).astype(F32)
    place_cols = (col_place[:, None] == jnp.arange(n_row, dtype=jnp.int32)[None, :]).astype(F32)
    order_cols = (col_index[:, None] == jnp.arange(n_row, dtype=jnp.int32)[None, :]).astype(F32)

    zl_blocks = lax.all_gather(features, "zl", axis=0, tiled=False)
    other_blocks = exchange(zl_blocks, "core")

    col_sums = jnp.sum(tile_vals[0, 0], axis=1, dtype=F32) * alive.astype(F32)[:, None]
    degree_terms = jnp.einsum("sc,sj->cj", order_cols, col_sums, precision=lax.Precision.HIGHEST)
    col_degree = 1.0 + jnp.sum(gather_copies(degree_terms, ROW), axis=0)
    col_scale = lax.rsqrt(col_degree)
    own_scale = lax.dynamic_index_in_dim(
        col_scale, my_zl * n_core + my_core, axis=0, keepdims=False
    )

    picked = jnp.concatenate([zl_blocks, other_blocks], axis=0)[col_place]
    picked = (picked.astype(F32) * col_scale[col_index][:, :, None]).astype(BF16)
    products = jnp.einsum("sij,sjf->sif", weights, picked, preferred_element_type=F32)

    def forward_terms(half):
        place = place_rows[:, half * n_plane : (half + 1) * n_plane]
        terms = jnp.einsum("sr,sif->rif", place, products, precision=lax.Precision.HIGHEST)
        return terms.astype(BF16)

    far_sum = jnp.sum(scatter_parts(forward_terms(1), PLANE).astype(F32), axis=0)
    from_far = exchange(far_sum.astype(BF16), "zh")
    near_sum = jnp.sum(scatter_parts(forward_terms(0), PLANE).astype(F32), axis=0)
    own_total = near_sum + from_far.astype(F32)

    output, normed, grad_pre, grad_own = layer_rows(own_total, cotangent, weight)

    grad_far = exchange(grad_own, "zh")
    grad_group = jnp.concatenate(
        [gather_copies(grad_own, PLANE), gather_copies(grad_far, PLANE)], axis=0
    )

    weight_terms = jnp.einsum("nf,ng->fg", normed, grad_pre, preferred_element_type=F32)
    plane_part = scatter_parts(
        weight_terms.astype(BF16).reshape(n_plane, width // n_plane, width), PLANE
    )
    plane_sum = jnp.sum(plane_part.astype(F32), axis=0)
    depth = n_row * n_zh
    depth_part = scatter_parts(plane_sum.reshape(depth, -1, 128), DEPTH)
    depth_sum = jnp.sum(depth_part, axis=0) * (1.0 / math.sqrt(nodes))
    plane_rows = gather_copies(depth_sum, DEPTH).reshape(width // n_plane, width)
    weight_grad = gather_copies(plane_rows, PLANE).reshape(width, width)

    grad_picked = grad_group[row_place]
    back_products = jnp.einsum("sij,sif->sjf", weights, grad_picked, preferred_element_type=F32)
    back_terms = jnp.einsum(
        "sc,sjf->cjf", place_cols, back_products, precision=lax.Precision.HIGHEST
    ).astype(BF16)
    core_sum = back_terms[:n_zl].astype(F32) + exchange(back_terms[n_zl:], "core").astype(F32)
    own_grad = jnp.sum(scatter_parts(core_sum.astype(BF16), "zl").astype(F32), axis=0)
    feature_grad = own_grad * own_scale[:, None]
    return (output, weight_grad, feature_grad)


def solution(mesh):
    fine = Mesh(mesh.devices.reshape(8, 2, 4, 2, 4), AXES)
    nodes, row, col = P(AXES, None), ("zl", "core"), ("y", "zh", "x")
    in_specs = (
        nodes,
        P(),
        nodes,
        P(row, col, None),
        P(row, col, None),
        P(row, col),
        P(row, col, None, None, None),
    )
    out_specs = (nodes, P(), nodes)
    return jax.shard_map(local, mesh=fine, in_specs=in_specs, out_specs=out_specs, check_vma=False)
```

```python
import math

import jax
import jax.numpy as jnp
from jax import lax
from jax.sharding import Mesh
from jax.sharding import PartitionSpec as P

AXES = ("zl", "core", "y", "zh", "x")
ROW = ("zl", "core")
PLANE = ("y", "x")
CHUNKS = 2
SHIFT = {1: 0, 2: 1, 4: 2}
BF16 = jnp.bfloat16
F32 = jnp.float32


def layer_rows(row_total, grad_rows, weight):
    inv_rms = lax.rsqrt(jnp.mean(row_total * row_total, axis=1, keepdims=True) + 1e-06)
    norm_f32 = row_total * inv_rms
    normed = norm_f32.astype(BF16)
    pre_act = jnp.dot(normed, weight, preferred_element_type=F32)
    output = jax.nn.silu(pre_act).astype(BF16)
    sigmoid_pre = jax.nn.sigmoid(pre_act)
    act_slope = sigmoid_pre * (1.0 + pre_act * (1.0 - sigmoid_pre))
    grad_pre = (grad_rows.astype(F32) * act_slope).astype(BF16)
    grad_norm = jnp.einsum("ng,fg->nf", grad_pre, weight, preferred_element_type=F32)
    grad_z = (
        inv_rms * (grad_norm - norm_f32 * jnp.mean(grad_norm * norm_f32, axis=1, keepdims=True))
    ).astype(BF16)
    return (output, normed, grad_pre, grad_z)


def flip(block, axis, distance):
    count = lax.axis_size(axis)
    return lax.ppermute(block, axis, [(i, i ^ distance) for i in range(count)])


def scatter_parts(parts, axes):
    return lax.all_to_all(parts, axes, split_axis=0, concat_axis=0, tiled=True)


def gather_copies(block, axes):
    count = lax.axis_size(axes)
    copies = jnp.broadcast_to(block[None], (count,) + block.shape)
    return lax.all_to_all(copies, axes, split_axis=0, concat_axis=0, tiled=True)


def keep_and_send(block, bit):
    halves = block.reshape((2, block.shape[0] // 2) + block.shape[1:])
    keep = lax.dynamic_index_in_dim(halves, bit, axis=0, keepdims=False)
    send = lax.dynamic_index_in_dim(halves, 1 - bit, axis=0, keepdims=False)
    return keep, send


def total_everywhere(block):
    steps = (("x", 1), ("y", 1), ("x", 2), ("y", 2))
    for number, (axis, distance) in enumerate(steps):
        bit = (lax.axis_index(axis) >> SHIFT[distance]) & 1
        keep, send = keep_and_send(block, bit)
        send = send.astype(BF16) if number < 2 else send
        block = keep + flip(send, axis, distance).astype(F32)
    for axis, distance in (("core", 1), ("zl", 1), ("zl", 2), ("zl", 4), ("zh", 1)):
        block = block + flip(block, axis, distance)
    for axis, distance in reversed(steps):
        bit = (lax.axis_index(axis) >> SHIFT[distance]) & 1
        other = flip(block, axis, distance)
        block = jnp.where(
            bit == 0, jnp.concatenate([block, other]), jnp.concatenate([other, block])
        )
    return block


def local(features, weight, cotangent, tile_rows, tile_cols, tile_count, tile_vals):
    span, width = features.shape
    n_zl, n_core = lax.axis_size("zl"), lax.axis_size("core")
    n_y, n_zh, n_x = lax.axis_size("y"), lax.axis_size("zh"), lax.axis_size("x")
    n_row, n_col = n_zl * n_core, n_y * n_zh * n_x
    n_plane = n_y * n_x
    my_zl, my_core, my_zh = lax.axis_index("zl"), lax.axis_index("core"), lax.axis_index("zh")
    slots = tile_vals.shape[2]
    nodes = n_row * n_col * span
    chunk = width // CHUNKS
    alive = jnp.arange(slots, dtype=jnp.int32) < tile_count[0, 0]
    weights = tile_vals[0, 0] * alive.astype(BF16)[:, None, None]
    row_index = tile_rows[0, 0]
    col_index = tile_cols[0, 0]
    zl_bits = (col_index // n_core) ^ my_zl
    zl_place = (zl_bits & 1) * 4 + (zl_bits & 2) + zl_bits // 4
    col_place = ((col_index % n_core) ^ my_core) * n_zl + zl_place
    row_plane = (row_index // (n_zh * n_x)) * n_x + row_index % n_x
    row_place = (((row_index // n_x) % n_zh) ^ my_zh) * n_plane + row_plane
    place_rows = (row_place[:, None] == jnp.arange(n_col, dtype=jnp.int32)[None, :]).astype(F32)
    place_cols = (col_place[:, None] == jnp.arange(n_row, dtype=jnp.int32)[None, :]).astype(F32)
    order_cols = (col_index[:, None] == jnp.arange(n_row, dtype=jnp.int32)[None, :]).astype(F32)
    parts = [slice(c * chunk, (c + 1) * chunk) for c in range(CHUNKS)]

    col_sums = jnp.sum(tile_vals[0, 0], axis=1, dtype=F32) * alive.astype(F32)[:, None]
    degree_terms = jnp.einsum("sc,sj->cj", order_cols, col_sums, precision=lax.Precision.HIGHEST)
    col_degree = 1.0 + jnp.sum(gather_copies(degree_terms, ROW), axis=0)
    col_scale = lax.rsqrt(col_degree)
    own_scale = lax.dynamic_index_in_dim(
        col_scale, my_zl * n_core + my_core, axis=0, keepdims=False
    )
    slot_scale = col_scale[col_index][:, :, None]

    far_sums, near_sums, forward = [], [], []
    for part in parts:
        blocks = features[:, part][None]
        for axis, distance in (("zl", 4), ("zl", 2), ("zl", 1), ("core", 1)):
            blocks = jnp.concatenate([blocks, flip(blocks, axis, distance)])
        picked = (blocks[col_place].astype(F32) * slot_scale).astype(BF16)
        products = jnp.einsum("sij,sjf->sif", weights, picked, preferred_element_type=F32)
        terms = jnp.einsum("sr,sif->rif", place_rows, products, precision=lax.Precision.HIGHEST)
        forward.append(terms.astype(BF16))
    for terms in forward:
        far = jnp.sum(scatter_parts(terms[n_plane:], PLANE).astype(F32), axis=0)
        far_sums.append(flip(far.astype(BF16), "zh", 1))
    for terms in forward:
        near_sums.append(jnp.sum(scatter_parts(terms[:n_plane], PLANE).astype(F32), axis=0))
    own_total = jnp.concatenate(
        [near + far.astype(F32) for near, far in zip(near_sums, far_sums)], axis=1
    )

    output, normed, grad_pre, grad_own = layer_rows(own_total, cotangent, weight)

    grad_far = flip(grad_own, "zh", 1)
    weight_terms = jnp.einsum("nf,ng->fg", normed, grad_pre, preferred_element_type=F32)
    weight_grad = total_everywhere(weight_terms) * (1.0 / math.sqrt(nodes))

    own_grads = []
    for part in parts:
        grad_group = jnp.concatenate(
            [gather_copies(grad_own[:, part], PLANE), gather_copies(grad_far[:, part], PLANE)]
        )
        grad_picked = grad_group[row_place]
        back_products = jnp.einsum("sij,sif->sjf", weights, grad_picked, preferred_element_type=F32)
        total = jnp.einsum(
            "sc,sjf->cjf", place_cols, back_products, precision=lax.Precision.HIGHEST
        )
        for axis, distance in (("core", 1), ("zl", 1), ("zl", 2), ("zl", 4)):
            half = total.shape[0] // 2
            total = total[:half] + flip(total[half:].astype(BF16), axis, distance).astype(F32)
        own_grads.append(total[0])
    feature_grad = jnp.concatenate(own_grads, axis=1) * own_scale[:, None]
    return (output, weight_grad, feature_grad)


def solution(mesh):
    fine = Mesh(mesh.devices.reshape(8, 2, 4, 2, 4), AXES)
    nodes, row, col = P(AXES, None), ("zl", "core"), ("y", "zh", "x")
    in_specs = (
        nodes,
        P(),
        nodes,
        P(row, col, None),
        P(row, col, None),
        P(row, col),
        P(row, col, None, None, None),
    )
    out_specs = (nodes, P(), nodes)
    return jax.shard_map(local, mesh=fine, in_specs=in_specs, out_specs=out_specs, check_vma=False)
```

```python
import functools
import math

import jax
import jax.numpy as jnp
from jax import lax
from jax.experimental import pallas as pl
from jax.experimental.pallas import tpu as pltpu
from jax.sharding import Mesh
from jax.sharding import PartitionSpec as P

AXES = ("z4", "z1", "core", "y", "zh", "x")
LINE = ("z4", "z1")
ROW = ("z4", "z1", "core")
PLANE = ("y", "x")
DEPTH = ("z4", "z1", "core", "zh")
CHUNKS = 2
BF16 = jnp.bfloat16
F32 = jnp.float32


def layer_rows(row_total, grad_rows, weight):
    inv_rms = lax.rsqrt(jnp.mean(row_total * row_total, axis=1, keepdims=True) + 1e-06)
    norm_f32 = row_total * inv_rms
    normed = norm_f32.astype(BF16)
    pre_act = jnp.dot(normed, weight, preferred_element_type=F32)
    output = jax.nn.silu(pre_act).astype(BF16)
    sigmoid_pre = jax.nn.sigmoid(pre_act)
    act_slope = sigmoid_pre * (1.0 + pre_act * (1.0 - sigmoid_pre))
    grad_pre = (grad_rows.astype(F32) * act_slope).astype(BF16)
    grad_norm = jnp.einsum("ng,fg->nf", grad_pre, weight, preferred_element_type=F32)
    grad_z = (
        inv_rms * (grad_norm - norm_f32 * jnp.mean(grad_norm * norm_f32, axis=1, keepdims=True))
    ).astype(BF16)
    return (output, normed, grad_pre, grad_z)


def flip(block, axis):
    return lax.ppermute(block, axis, [(0, 1), (1, 0)])


def after(value, *others):
    return lax.optimization_barrier((value,) + others)[0]


def swap_parts(parts, axes):
    return lax.all_to_all(parts, axes, split_axis=0, concat_axis=0, tiled=True)


def copies_of(block, axes):
    return jnp.broadcast_to(block[None], (lax.axis_size(axes),) + block.shape)


def tile_kernel(
    transposed, slots, source, target, count, tiles, scale, first, second, near, far, total
):
    half = first.shape[0]
    near_blocks = near.shape[0]
    total[...] = jnp.zeros_like(total)
    for slot in range(slots):

        @pl.when(slot < count[0])
        def _():
            place = source[slot]
            tile = tiles[slot]

            def add(block):
                if scale is not None:
                    row = jnp.broadcast_to(scale[slot : slot + 1, :], (tile.shape[1], tile.shape[1]))
                    column = jnp.transpose(row)
                    lanes = column.shape[1]
                    block = jnp.concatenate(
                        [
                            (block[:, i : i + lanes].astype(F32) * column).astype(BF16)
                            for i in range(0, block.shape[1], lanes)
                        ],
                        axis=1,
                    )
                axis = 0 if transposed else 1
                total[target[slot]] += lax.dot_general(
                    tile, block, (((axis,), (0,)), ((), ())), preferred_element_type=F32
                )

            @pl.when(place < half)
            def _():
                add(first[jnp.minimum(place, half - 1), : tile.shape[0], :])

            @pl.when(place >= half)
            def _():
                add(second[jnp.maximum(place - half, 0), : tile.shape[0], :])

    near[...] = total[:near_blocks].astype(BF16)
    far[...] = total[near_blocks:].astype(BF16)


def tile_sums(transposed, source, target, count, tiles, scale, first, second, blocks):
    slots, size, _ = tiles.shape
    width = first.shape[2]
    smem = pl.BlockSpec(memory_space=pltpu.SMEM)
    vmem = pl.BlockSpec(memory_space=pltpu.VMEM)
    half = jax.ShapeDtypeStruct((blocks // 2, size, width), BF16)
    operands = [source, target, count, tiles]
    specs = [smem, smem, smem, vmem]
    kernel = functools.partial(tile_kernel, transposed, slots)
    if scale is None:
        body = lambda s, t, c, w, *refs: kernel(s, t, c, w, None, *refs)
    else:
        body = kernel
        operands, specs = operands + [scale], specs + [vmem]
    return pl.pallas_call(
        body,
        out_shape=(half, half),
        in_specs=specs + [vmem, vmem],
        out_specs=(vmem, vmem),
        scratch_shapes=[pltpu.VMEM((blocks, size, width), F32)],
        compiler_params=pltpu.CompilerParams(vmem_limit_bytes=40 * 1024 * 1024),
        cost_estimate=pl.CostEstimate(
            flops=2 * slots * size * size * width,
            bytes_accessed=6 * blocks * size * width,
            transcendentals=0,
        ),
    )(*operands, first, second)


def local(features, weight, cotangent, tile_rows, tile_cols, tile_count, tile_vals):
    span, width = features.shape
    n_z4, n_z1, n_core = lax.axis_size("z4"), lax.axis_size("z1"), lax.axis_size("core")
    n_y, n_zh, n_x = lax.axis_size("y"), lax.axis_size("zh"), lax.axis_size("x")
    n_line = n_z4 * n_z1
    n_row, n_col = n_line * n_core, n_y * n_zh * n_x
    n_plane = n_y * n_x
    my_row = lax.axis_index(ROW)
    my_z1, my_core, my_zh = lax.axis_index("z1"), lax.axis_index("core"), lax.axis_index("zh")
    slots = tile_vals.shape[2]
    nodes = n_row * n_col * span
    chunk = width // CHUNKS
    parts = [slice(c * chunk, (c + 1) * chunk) for c in range(CHUNKS)]
    tiles = tile_vals[0, 0]
    count = tile_count[0]
    row_index = tile_rows[0, 0]
    col_index = tile_cols[0, 0]
    col_core = (col_index & 1) ^ my_core
    col_from = col_core * n_line + (col_index >> 1)
    col_to = col_core * n_line + (((col_index >> 1) & 1) ^ my_z1) * n_z4 + (col_index >> 2)
    row_plane = (row_index >> 3) * n_x + (row_index & 3)
    row_place = (((row_index >> 2) & 1) ^ my_zh) * n_plane + row_plane

    alive = (jnp.arange(slots, dtype=jnp.int32) < count[0]).astype(F32)
    order_cols = (col_index[:, None] == jnp.arange(n_row, dtype=jnp.int32)[None, :]).astype(F32)
    col_sums = jnp.sum(tiles, axis=1, dtype=F32) * alive[:, None]
    degree_terms = jnp.einsum("sc,sj->cj", order_cols, col_sums, precision=lax.Precision.HIGHEST)
    col_degree = 1.0 + lax.psum(degree_terms.reshape(n_row * span), ROW).reshape(n_row, span)
    col_scale = lax.rsqrt(col_degree)
    own_scale = lax.dynamic_index_in_dim(col_scale, my_row, axis=0, keepdims=False)
    slot_scale = col_scale[col_index]
    first_part, second_part = (features[:, part] for part in parts)
    line_blocks = [
        swap_parts(copies_of(part, LINE), LINE)
        for part in (first_part, after(second_part, col_scale))
    ]

    near_terms, far_terms = [], []
    for blocks in line_blocks:
        near, far = tile_sums(
            False, col_from, row_place, count, tiles, slot_scale, blocks, flip(blocks, "core"), n_col
        )
        near_terms.append(near)
        far_terms.append(far)
    far_sums = [
        jnp.sum(swap_parts(terms, PLANE).astype(F32), axis=0).astype(BF16) for terms in far_terms
    ]
    from_far = [flip(total, "zh") for total in far_sums]
    near_terms[0] = after(near_terms[0], far_sums[0])
    near_terms[1] = after(near_terms[1], far_sums[1], from_far[0])
    near_sums = [jnp.sum(swap_parts(terms, PLANE).astype(F32), axis=0) for terms in near_terms]
    own_total = jnp.concatenate(
        [near + far.astype(F32) for near, far in zip(near_sums, from_far)], axis=1
    )

    output, normed, grad_pre, grad_own = layer_rows(own_total, cotangent, weight)

    weight_terms = jnp.einsum("nf,ng->fg", normed, grad_pre, preferred_element_type=F32)
    weight_parts = weight_terms.astype(BF16).reshape(n_plane, width // n_plane, width)
    near_group = swap_parts(
        jnp.concatenate([copies_of(grad_own, PLANE), weight_parts], axis=1), PLANE
    )
    far_group = swap_parts(copies_of(after(flip(grad_own, "zh"), near_group), PLANE), PLANE)

    depth = n_row * n_zh
    plane_sum = jnp.sum(near_group[:, span:].astype(F32), axis=0)
    plane_sum = after(plane_sum, far_group)
    depth_part = swap_parts(plane_sum.reshape(depth, -1, 128), DEPTH)
    depth_sum = jnp.sum(depth_part, axis=0) * (1.0 / math.sqrt(nodes))

    near, far = tile_sums(
        True, row_place, col_to, count, tiles, None, near_group, far_group, n_row
    )
    core_sum = (near.astype(F32) + flip(far, "core").astype(F32)).astype(BF16)
    pair_far = flip(after(core_sum[n_z4:], depth_sum), "z1")
    pair_sum = (core_sum[:n_z4].astype(F32) + pair_far.astype(F32)).astype(BF16)
    depth_sum = after(depth_sum, pair_sum)
    own_grad = lax.psum_scatter(pair_sum, "z4", scatter_dimension=0, tiled=False)
    feature_grad = own_grad.astype(F32) * own_scale[:, None]

    depth_rows = swap_parts(copies_of(depth_sum, DEPTH), DEPTH).reshape(width // n_plane, width)
    weight_grad = swap_parts(copies_of(depth_rows, PLANE), PLANE).reshape(width, width)
    return (output, weight_grad, feature_grad)


def solution(mesh):
    fine = Mesh(mesh.devices.reshape(4, 2, 2, 4, 2, 4), AXES)
    nodes, row, col = P(AXES, None), ROW, ("y", "zh", "x")
    in_specs = (
        nodes,
        P(),
        nodes,
        P(row, col, None),
        P(row, col, None),
        P(row, col),
        P(row, col, None, None, None),
    )
    out_specs = (nodes, P(), nodes)
    return jax.shard_map(local, mesh=fine, in_specs=in_specs, out_specs=out_specs, check_vma=False)
```

```python
import functools
import math

import jax
import jax.numpy as jnp
from jax import lax
from jax.experimental import pallas as pl
from jax.experimental.pallas import tpu as pltpu
from jax.sharding import Mesh
from jax.sharding import PartitionSpec as P

AXES = ("z4", "z1", "core", "y", "zh", "x")
LINE = ("z4", "z1")
ROW = ("z4", "z1", "core")
PLANE = ("y", "x")
DEPTH = ("z4", "z1", "core", "zh")
BF16 = jnp.bfloat16
F32 = jnp.float32


def layer_rows(row_total, grad_rows, weight):
    inv_rms = lax.rsqrt(jnp.mean(row_total * row_total, axis=1, keepdims=True) + 1e-06)
    norm_f32 = row_total * inv_rms
    normed = norm_f32.astype(BF16)
    pre_act = jnp.dot(normed, weight, preferred_element_type=F32)
    output = jax.nn.silu(pre_act).astype(BF16)
    sigmoid_pre = jax.nn.sigmoid(pre_act)
    act_slope = sigmoid_pre * (1.0 + pre_act * (1.0 - sigmoid_pre))
    grad_pre = (grad_rows.astype(F32) * act_slope).astype(BF16)
    grad_norm = jnp.einsum("ng,fg->nf", grad_pre, weight, preferred_element_type=F32)
    grad_z = (
        inv_rms * (grad_norm - norm_f32 * jnp.mean(grad_norm * norm_f32, axis=1, keepdims=True))
    ).astype(BF16)
    return (output, normed, grad_pre, grad_z)


def flip(block, axis):
    return lax.ppermute(block, axis, [(0, 1), (1, 0)])


def after(value, *others):
    return lax.optimization_barrier((value,) + others)[0]


def swap_parts(parts, axes):
    return lax.all_to_all(parts, axes, split_axis=0, concat_axis=0, tiled=True)


def copies_of(block, axes):
    return jnp.broadcast_to(block[None], (lax.axis_size(axes),) + block.shape)


def tile_kernel(
    transposed, slots, source, target, count, tiles, scale, first, second, near, far, total
):
    half = first.shape[0]
    near_blocks = near.shape[0]
    total[...] = jnp.zeros_like(total)
    for slot in range(slots):

        @pl.when(slot < count[0])
        def _():
            place = source[slot]
            tile = tiles[slot]

            def add(block):
                if scale is not None:
                    row = jnp.broadcast_to(scale[slot : slot + 1, :], (tile.shape[1], tile.shape[1]))
                    column = jnp.transpose(row)
                    lanes = column.shape[1]
                    block = jnp.concatenate(
                        [
                            (block[:, i : i + lanes].astype(F32) * column).astype(BF16)
                            for i in range(0, block.shape[1], lanes)
                        ],
                        axis=1,
                    )
                axis = 0 if transposed else 1
                total[target[slot]] += lax.dot_general(
                    tile, block, (((axis,), (0,)), ((), ())), preferred_element_type=F32
                )

            @pl.when(place < half)
            def _():
                add(first[jnp.minimum(place, half - 1), : tile.shape[0], :])

            @pl.when(place >= half)
            def _():
                add(second[jnp.maximum(place - half, 0), : tile.shape[0], :])

    near[...] = total[:near_blocks].astype(BF16)
    far[...] = total[near_blocks:].astype(BF16)


def tile_sums(transposed, source, target, count, tiles, scale, first, second, blocks):
    slots, size, _ = tiles.shape
    width = first.shape[2]
    smem = pl.BlockSpec(memory_space=pltpu.SMEM)
    vmem = pl.BlockSpec(memory_space=pltpu.VMEM)
    half = jax.ShapeDtypeStruct((blocks // 2, size, width), BF16)
    operands = [source, target, count, tiles]
    specs = [smem, smem, smem, vmem]
    kernel = functools.partial(tile_kernel, transposed, slots)
    if scale is None:
        body = lambda s, t, c, w, *refs: kernel(s, t, c, w, None, *refs)
    else:
        body = kernel
        operands, specs = operands + [scale], specs + [vmem]
    return pl.pallas_call(
        body,
        out_shape=(half, half),
        in_specs=specs + [vmem, vmem],
        out_specs=(vmem, vmem),
        scratch_shapes=[pltpu.VMEM((blocks, size, width), F32)],
        compiler_params=pltpu.CompilerParams(vmem_limit_bytes=40 * 1024 * 1024),
        cost_estimate=pl.CostEstimate(
            flops=2 * slots * size * size * width,
            bytes_accessed=6 * blocks * size * width,
            transcendentals=0,
        ),
    )(*operands, first, second)


def local(features, weight, cotangent, tile_rows, tile_cols, tile_count, tile_vals):
    span, width = features.shape
    n_z4, n_z1, n_core = lax.axis_size("z4"), lax.axis_size("z1"), lax.axis_size("core")
    n_y, n_zh, n_x = lax.axis_size("y"), lax.axis_size("zh"), lax.axis_size("x")
    n_line = n_z4 * n_z1
    n_row, n_col = n_line * n_core, n_y * n_zh * n_x
    n_plane = n_y * n_x
    my_row = lax.axis_index(ROW)
    my_z1, my_core, my_zh = lax.axis_index("z1"), lax.axis_index("core"), lax.axis_index("zh")
    slots = tile_vals.shape[2]
    nodes = n_row * n_col * span
    tiles = tile_vals[0, 0]
    count = tile_count[0]
    row_index = tile_rows[0, 0]
    col_index = tile_cols[0, 0]
    col_core = (col_index & 1) ^ my_core
    col_from = col_core * n_line + (col_index >> 1)
    col_to = col_core * n_line + (((col_index >> 1) & 1) ^ my_z1) * n_z4 + (col_index >> 2)
    row_plane = (row_index >> 3) * n_x + (row_index & 3)
    row_place = (((row_index >> 2) & 1) ^ my_zh) * n_plane + row_plane

    alive = (jnp.arange(slots, dtype=jnp.int32) < count[0]).astype(F32)
    order_cols = (col_index[:, None] == jnp.arange(n_row, dtype=jnp.int32)[None, :]).astype(F32)
    col_sums = jnp.sum(tiles, axis=1, dtype=F32) * alive[:, None]
    degree_terms = jnp.einsum("sc,sj->cj", order_cols, col_sums, precision=lax.Precision.HIGHEST)
    high = lax.reduce_precision(degree_terms, 8, 7)
    middle = lax.reduce_precision(degree_terms - high, 8, 7)
    pieces = jnp.stack([high, middle, degree_terms - high - middle]).astype(BF16)
    pieces = pieces.reshape(-1, width)
    extra = pieces.shape[0]
    pieces = jnp.pad(pieces, ((0, -extra % 16), (0, 0)))
    line_blocks = swap_parts(copies_of(jnp.concatenate([features, pieces]), LINE), LINE)
    other_blocks = flip(line_blocks, "core")

    def degrees(blocks):
        terms = blocks[:, span : span + extra].astype(F32)
        return jnp.sum(terms.reshape(n_line * 3, n_row, span), axis=0)

    col_scale = lax.rsqrt(1.0 + degrees(line_blocks) + degrees(other_blocks))
    own_scale = lax.dynamic_index_in_dim(col_scale, my_row, axis=0, keepdims=False)
    slot_scale = col_scale[col_index]

    near_terms, far_terms = tile_sums(
        False, col_from, row_place, count, tiles, slot_scale, line_blocks, other_blocks, n_col
    )
    far_sum = jnp.sum(swap_parts(far_terms, PLANE).astype(F32), axis=0).astype(BF16)
    near_group = swap_parts(after(near_terms, far_sum), PLANE)
    own_total = jnp.sum(near_group.astype(F32), axis=0) + flip(far_sum, "zh").astype(F32)

    output, normed, grad_pre, grad_own = layer_rows(own_total, cotangent, weight)

    weight_terms = jnp.einsum("nf,ng->fg", normed, grad_pre, preferred_element_type=F32)
    weight_parts = weight_terms.astype(BF16).reshape(n_plane, width // n_plane, width)
    near_group = swap_parts(
        jnp.concatenate([copies_of(grad_own, PLANE), weight_parts], axis=1), PLANE
    )
    far_group = swap_parts(copies_of(after(flip(grad_own, "zh"), near_group), PLANE), PLANE)

    depth = n_row * n_zh
    plane_sum = jnp.sum(near_group[:, span:].astype(F32), axis=0)
    plane_sum, far_group = lax.optimization_barrier((plane_sum, far_group))
    depth_part = swap_parts(plane_sum.reshape(depth, -1, 128), DEPTH)
    depth_sum = jnp.sum(depth_part, axis=0) * (1.0 / math.sqrt(nodes))

    near, far = tile_sums(
        True, row_place, col_to, count, tiles, None, near_group, far_group, n_row
    )
    core_sum = (near.astype(F32) + flip(far, "core").astype(F32)).astype(BF16)
    pair_far = flip(core_sum[n_z4:], "z1")
    pair_sum = (core_sum[:n_z4].astype(F32) + pair_far.astype(F32)).astype(BF16)
    depth_sum = after(depth_sum, pair_sum)
    own_grad = lax.psum_scatter(pair_sum, "z4", scatter_dimension=0, tiled=False)
    feature_grad = own_grad.astype(F32) * own_scale[:, None]

    depth_rows = swap_parts(copies_of(depth_sum, DEPTH), DEPTH).reshape(width // n_plane, width)
    weight_grad = swap_parts(copies_of(depth_rows, PLANE), PLANE).reshape(width, width)
    return (output, weight_grad, feature_grad)


def solution(mesh):
    fine = Mesh(mesh.devices.reshape(4, 2, 2, 4, 2, 4), AXES)
    nodes, row, col = P(AXES, None), ROW, ("y", "zh", "x")
    in_specs = (
        nodes,
        P(),
        nodes,
        P(row, col, None),
        P(row, col, None),
        P(row, col),
        P(row, col, None, None, None),
    )
    out_specs = (nodes, P(), nodes)
    return jax.shard_map(local, mesh=fine, in_specs=in_specs, out_specs=out_specs, check_vma=False)
```

```python
import functools
import math

import jax
import jax.numpy as jnp
from jax import lax
from jax.experimental import pallas as pl
from jax.experimental.pallas import tpu as pltpu
from jax.sharding import Mesh
from jax.sharding import PartitionSpec as P

AXES = ("z4", "z1", "core", "y", "zh", "x")
ROW = ("z4", "z1", "core")
PLANE = ("y", "x")
BF16 = jnp.bfloat16
F32 = jnp.float32


def layer_rows(row_total, grad_rows, weight):
    inv_rms = lax.rsqrt(jnp.mean(row_total * row_total, axis=1, keepdims=True) + 1e-06)
    norm_f32 = row_total * inv_rms
    normed = norm_f32.astype(BF16)
    pre_act = jnp.dot(normed, weight, preferred_element_type=F32)
    output = jax.nn.silu(pre_act).astype(BF16)
    sigmoid_pre = jax.nn.sigmoid(pre_act)
    act_slope = sigmoid_pre * (1.0 + pre_act * (1.0 - sigmoid_pre))
    grad_pre = (grad_rows.astype(F32) * act_slope).astype(BF16)
    grad_norm = jnp.einsum("ng,fg->nf", grad_pre, weight, preferred_element_type=F32)
    grad_z = (
        inv_rms * (grad_norm - norm_f32 * jnp.mean(grad_norm * norm_f32, axis=1, keepdims=True))
    ).astype(BF16)
    return (output, normed, grad_pre, grad_z)


def flip(block, axis):
    return lax.ppermute(block, axis, [(0, 1), (1, 0)])


def after(value, *others):
    return lax.optimization_barrier((value,) + others)[0]


def swap_parts(parts, axes):
    return lax.all_to_all(parts, axes, split_axis=0, concat_axis=0, tiled=True)


def copies_of(block, axes):
    return jnp.broadcast_to(block[None], (lax.axis_size(axes),) + block.shape)


def tile_kernel(transposed, scaled, source, target, count, tiles, *refs):
    scale, refs = (refs[0], refs[1:]) if scaled else (None, refs)
    *groups, near, far, total = refs
    slots, size, _ = tiles.shape
    held, near_blocks = groups[0].shape[0], near.shape[0]
    axis = 0 if transposed else 1
    total[...] = jnp.zeros_like(total)
    for slot in range(slots):

        def add(block):
            if scaled:
                row = jnp.broadcast_to(scale[slot : slot + 1, :], (size, size))
                column = jnp.transpose(row)
                lanes = [block[:, i : i + size] for i in range(0, block.shape[1], size)]
                lanes = [(part.astype(F32) * column).astype(BF16) for part in lanes]
                block = jnp.concatenate(lanes, axis=1)
            total[target[slot]] += lax.dot_general(
                tiles[slot], block, (((axis,), (0,)), ((), ())), preferred_element_type=F32
            )

        for number, group in enumerate(groups):
            inside = source[slot] - number * held

            @pl.when((slot < count[0]) & (inside >= 0) & (inside < held))
            def _(group=group, inside=inside):
                add(group[jnp.clip(inside, 0, held - 1), :size, :])

    near[...] = total[:near_blocks].astype(BF16)
    far[...] = total[near_blocks:].astype(BF16)


def tile_sums(transposed, source, target, count, tiles, scale, groups, blocks):
    slots, size, _ = tiles.shape
    width = groups[0].shape[2]
    smem = pl.BlockSpec(memory_space=pltpu.SMEM)
    vmem = pl.BlockSpec(memory_space=pltpu.VMEM)
    half = jax.ShapeDtypeStruct((blocks // 2, size, width), BF16)
    scaled = scale is not None
    operands = [tiles] + [scale] * scaled + list(groups)
    return pl.pallas_call(
        functools.partial(tile_kernel, transposed, scaled),
        out_shape=(half, half),
        in_specs=[smem] * 3 + [vmem] * len(operands),
        out_specs=(vmem, vmem),
        scratch_shapes=[pltpu.VMEM((blocks, size, width), F32)],
        compiler_params=pltpu.CompilerParams(vmem_limit_bytes=40 * 1024 * 1024),
        cost_estimate=pl.CostEstimate(
            flops=2 * slots * size * size * width,
            bytes_accessed=6 * blocks * size * width,
            transcendentals=0,
        ),
    )(source, target, count, *operands)


def local(features, weight, cotangent, tile_rows, tile_cols, tile_count, tile_vals):
    span, width = features.shape
    n_z4, n_z1, n_core = lax.axis_size("z4"), lax.axis_size("z1"), lax.axis_size("core")
    n_y, n_zh, n_x = lax.axis_size("y"), lax.axis_size("zh"), lax.axis_size("x")
    n_line = n_z4 * n_z1
    n_row, n_col = n_line * n_core, n_y * n_zh * n_x
    n_plane = n_y * n_x
    my_row = lax.axis_index(ROW)
    my_z1, my_core, my_zh = lax.axis_index("z1"), lax.axis_index("core"), lax.axis_index("zh")
    slots = tile_vals.shape[2]
    nodes = n_row * n_col * span
    tiles = tile_vals[0, 0]
    count = tile_count[0]
    row_index = tile_rows[0, 0]
    col_index = tile_cols[0, 0]
    col_core = (col_index & 1) ^ my_core
    col_place = col_core * n_line + (((col_index >> 1) & 1) ^ my_z1) * n_z4 + (col_index >> 2)
    row_plane = (row_index >> 3) * n_x + (row_index & 3)
    row_place = (((row_index >> 2) & 1) ^ my_zh) * n_plane + row_plane

    alive = (jnp.arange(slots, dtype=jnp.int32) < count[0]).astype(F32)
    order_cols = (col_index[:, None] == jnp.arange(n_row, dtype=jnp.int32)[None, :]).astype(F32)
    col_sums = jnp.sum(tiles, axis=1, dtype=F32) * alive[:, None]
    degree_terms = jnp.einsum("sc,sj->cj", order_cols, col_sums, precision=lax.Precision.HIGHEST)
    high = lax.reduce_precision(degree_terms, 8, 7)
    middle = lax.reduce_precision(degree_terms - high, 8, 7)
    pieces = jnp.stack([high, middle, degree_terms - high - middle]).astype(BF16)
    pieces = pieces.reshape(-1, width)
    extra = pieces.shape[0]
    pieces = jnp.pad(pieces, ((0, -extra % 16), (0, 0)))
    own_line = swap_parts(copies_of(jnp.concatenate([features, pieces]), "z4"), "z4")
    own_pair = flip(own_line, "z1")
    blocks = [own_line, own_pair, flip(own_line, "core"), flip(own_pair, "core")]

    def degrees(part):
        terms = part[:, span : span + extra].astype(F32)
        return jnp.sum(terms.reshape(n_z4 * 3, n_row, span), axis=0)

    col_scale = lax.rsqrt(1.0 + sum(degrees(part) for part in blocks))
    own_scale = lax.dynamic_index_in_dim(col_scale, my_row, axis=0, keepdims=False)
    slot_scale = col_scale[col_index]

    near_terms, far_terms = tile_sums(
        False, col_place, row_place, count, tiles, slot_scale, blocks, n_col
    )
    far_sum = jnp.sum(swap_parts(far_terms, PLANE).astype(F32), axis=0).astype(BF16)
    near_group = swap_parts(after(near_terms, far_sum), PLANE)
    own_total = jnp.sum(near_group.astype(F32), axis=0) + flip(far_sum, "zh").astype(F32)

    output, normed, grad_pre, grad_own = layer_rows(own_total, cotangent, weight)

    weight_terms = jnp.einsum("nf,ng->fg", normed, grad_pre, preferred_element_type=F32)
    weight_parts = weight_terms.astype(BF16).reshape(n_plane, width // n_plane, width)
    near_group = swap_parts(
        jnp.concatenate([copies_of(grad_own, PLANE), weight_parts], axis=1), PLANE
    )
    far_group = swap_parts(copies_of(after(flip(grad_own, "zh"), near_group), PLANE), PLANE)

    plane_sum = jnp.sum(near_group[:, span:].astype(F32), axis=0)
    for axis in ("core", "z1", "zh"):
        plane_sum = plane_sum + flip(plane_sum, axis)
    far_group = after(far_group, plane_sum)
    line_part = swap_parts(plane_sum.reshape(n_z4, -1, width), "z4")
    line_sum = jnp.sum(line_part, axis=0) * (1.0 / math.sqrt(nodes))

    near, far = tile_sums(
        True, row_place, col_place, count, tiles, None, [near_group, far_group], n_row
    )
    core_sum = (near.astype(F32) + flip(far, "core").astype(F32)).astype(BF16)
    pair_far = flip(core_sum[n_z4:], "z1")
    pair_sum = (core_sum[:n_z4].astype(F32) + pair_far.astype(F32)).astype(BF16)
    line_sum = after(line_sum, pair_sum)
    own_grad = lax.psum_scatter(pair_sum, "z4", scatter_dimension=0, tiled=False)
    feature_grad = own_grad.astype(F32) * own_scale[:, None]

    plane_rows = swap_parts(copies_of(line_sum, "z4"), "z4").reshape(-1, width)
    weight_grad = swap_parts(copies_of(plane_rows, PLANE), PLANE).reshape(width, width)
    return (output, weight_grad, feature_grad)


def solution(mesh):
    fine = Mesh(mesh.devices.reshape(4, 2, 2, 4, 2, 4), AXES)
    nodes, row, col = P(AXES, None), ROW, ("y", "zh", "x")
    in_specs = (
        nodes,
        P(),
        nodes,
        P(row, col, None),
        P(row, col, None),
        P(row, col),
        P(row, col, None, None, None),
    )
    out_specs = (nodes, P(), nodes)
    return jax.shard_map(local, mesh=fine, in_specs=in_specs, out_specs=out_specs, check_vma=False)
```

```python
import functools
import math

import jax
import jax.numpy as jnp
from jax import lax
from jax.experimental import pallas as pl
from jax.experimental.pallas import tpu as pltpu
from jax.sharding import Mesh
from jax.sharding import PartitionSpec as P

AXES = ("za", "zb", "z1", "core", "y", "zh", "x")
Z4 = ("za", "zb")
ROW = ("za", "zb", "z1", "core")
PLANE = ("y", "x")
BF16 = jnp.bfloat16
F32 = jnp.float32


def layer_rows(row_total, grad_rows, weight):
    inv_rms = lax.rsqrt(jnp.mean(row_total * row_total, axis=1, keepdims=True) + 1e-06)
    norm_f32 = row_total * inv_rms
    normed = norm_f32.astype(BF16)
    pre_act = jnp.dot(normed, weight, preferred_element_type=F32)
    output = jax.nn.silu(pre_act).astype(BF16)
    sigmoid_pre = jax.nn.sigmoid(pre_act)
    act_slope = sigmoid_pre * (1.0 + pre_act * (1.0 - sigmoid_pre))
    grad_pre = (grad_rows.astype(F32) * act_slope).astype(BF16)
    grad_norm = jnp.einsum("ng,fg->nf", grad_pre, weight, preferred_element_type=F32)
    grad_z = (
        inv_rms * (grad_norm - norm_f32 * jnp.mean(grad_norm * norm_f32, axis=1, keepdims=True))
    ).astype(BF16)
    return (output, normed, grad_pre, grad_z)


def flip(block, axis):
    return lax.ppermute(block, axis, [(0, 1), (1, 0)])


def after(value, *others):
    return lax.optimization_barrier((value,) + others)[0]


def swap_parts(parts, axes):
    return lax.all_to_all(parts, axes, split_axis=0, concat_axis=0, tiled=True)


def copies_of(block, axes):
    return jnp.broadcast_to(block[None], (lax.axis_size(axes),) + block.shape)


def tile_kernel(transposed, scaled, source, target, count, tiles, *refs):
    scale, refs = (refs[0], refs[1:]) if scaled else (None, refs)
    *groups, near, far, total = refs
    slots, size, _ = tiles.shape
    held, near_blocks = groups[0].shape[0], near.shape[0]
    axis = 0 if transposed else 1
    total[...] = jnp.zeros_like(total)
    for slot in range(slots):

        def add(block):
            if scaled:
                row = jnp.broadcast_to(scale[slot : slot + 1, :], (size, size))
                column = jnp.transpose(row)
                lanes = [block[:, i : i + size] for i in range(0, block.shape[1], size)]
                lanes = [(part.astype(F32) * column).astype(BF16) for part in lanes]
                block = jnp.concatenate(lanes, axis=1)
            total[target[slot]] += lax.dot_general(
                tiles[slot], block, (((axis,), (0,)), ((), ())), preferred_element_type=F32
            )

        for number, group in enumerate(groups):
            inside = source[slot] - number * held

            @pl.when((slot < count[0]) & (inside >= 0) & (inside < held))
            def _(group=group, inside=inside):
                add(group[jnp.clip(inside, 0, held - 1), :size, :])

    near[...] = total[:near_blocks].astype(BF16)
    far[...] = total[near_blocks:].astype(BF16)


def tile_sums(transposed, source, target, count, tiles, scale, groups, blocks):
    slots, size, _ = tiles.shape
    width = groups[0].shape[2]
    smem = pl.BlockSpec(memory_space=pltpu.SMEM)
    vmem = pl.BlockSpec(memory_space=pltpu.VMEM)
    half = jax.ShapeDtypeStruct((blocks // 2, size, width), BF16)
    scaled = scale is not None
    operands = [tiles] + [scale] * scaled + list(groups)
    return pl.pallas_call(
        functools.partial(tile_kernel, transposed, scaled),
        out_shape=(half, half),
        in_specs=[smem] * 3 + [vmem] * len(operands),
        out_specs=(vmem, vmem),
        scratch_shapes=[pltpu.VMEM((blocks, size, width), F32)],
        compiler_params=pltpu.CompilerParams(vmem_limit_bytes=40 * 1024 * 1024),
        cost_estimate=pl.CostEstimate(
            flops=2 * slots * size * size * width,
            bytes_accessed=6 * blocks * size * width,
            transcendentals=0,
        ),
    )(source, target, count, *operands)


def local(features, weight, cotangent, tile_rows, tile_cols, tile_count, tile_vals):
    span, width = features.shape
    n_z4, n_z1, n_core = lax.axis_size(Z4), lax.axis_size("z1"), lax.axis_size("core")
    n_y, n_zh, n_x = lax.axis_size("y"), lax.axis_size("zh"), lax.axis_size("x")
    n_line = n_z4 * n_z1
    n_row, n_col = n_line * n_core, n_y * n_zh * n_x
    n_plane = n_y * n_x
    my_row = lax.axis_index(ROW)
    my_zh = lax.axis_index("zh")
    slots = tile_vals.shape[2]
    nodes = n_row * n_col * span
    tiles = tile_vals[0, 0]
    count = tile_count[0]
    row_index = tile_rows[0, 0]
    col_index = tile_cols[0, 0]
    col_bits = col_index ^ my_row
    col_near = (col_bits & 1) * n_line + (col_bits & 2) * (n_z4 // 2)
    col_from = col_near + (col_index >> 2)
    col_to = col_near + ((col_bits >> 2) & 1) * 2 + (col_bits >> 3)
    row_plane = (row_index >> 3) * n_x + (row_index & 3)
    row_place = (((row_index >> 2) & 1) ^ my_zh) * n_plane + row_plane

    alive = (jnp.arange(slots, dtype=jnp.int32) < count[0]).astype(F32)
    order_cols = (col_index[:, None] == jnp.arange(n_row, dtype=jnp.int32)[None, :]).astype(F32)
    col_sums = jnp.sum(tiles, axis=1, dtype=F32) * alive[:, None]
    degree_terms = jnp.einsum("sc,sj->cj", order_cols, col_sums, precision=lax.Precision.HIGHEST)
    high = lax.reduce_precision(degree_terms, 8, 7)
    pieces = jnp.stack([high, degree_terms - high]).astype(BF16).reshape(-1, width)
    own_line = swap_parts(copies_of(jnp.concatenate([features, pieces]), Z4), Z4)
    own_pair = flip(own_line, "z1")
    blocks = [own_line, own_pair, flip(own_line, "core"), flip(own_pair, "core")]

    def degrees(part):
        return jnp.sum(part[:, span:].astype(F32).reshape(-1, n_row, span), axis=0)

    col_scale = lax.rsqrt(1.0 + sum(degrees(part) for part in blocks))
    own_scale = lax.dynamic_index_in_dim(col_scale, my_row, axis=0, keepdims=False)
    slot_scale = col_scale[col_index]

    near_terms, far_terms = tile_sums(
        False, col_from, row_place, count, tiles, slot_scale, blocks, n_col
    )
    far_sum = jnp.sum(swap_parts(far_terms, PLANE).astype(F32), axis=0).astype(BF16)
    near_group = swap_parts(after(near_terms, far_sum), PLANE)
    own_total = jnp.sum(near_group.astype(F32), axis=0) + flip(far_sum, "zh").astype(F32)

    output, normed, grad_pre, grad_own = layer_rows(own_total, cotangent, weight)

    weight_terms = jnp.einsum("nf,ng->fg", normed, grad_pre, preferred_element_type=F32)
    weight_parts = weight_terms.astype(BF16).reshape(n_plane, width // n_plane, width)
    near_group = swap_parts(
        jnp.concatenate([copies_of(grad_own, PLANE), weight_parts], axis=1), PLANE
    )
    far_group = swap_parts(copies_of(after(flip(grad_own, "zh"), near_group), PLANE), PLANE)

    plane_sum = jnp.sum(near_group[:, span:].astype(F32), axis=0)
    for axis in ("core", "z1", "zh"):
        plane_sum = plane_sum + flip(plane_sum, axis)
    far_group = after(far_group, plane_sum)
    line_part = swap_parts(plane_sum.reshape(n_z4, -1, width), Z4)
    line_sum = jnp.sum(line_part, axis=0) * (1.0 / math.sqrt(nodes))

    near, far = tile_sums(
        True, row_place, col_to, count, tiles, None, [near_group, far_group], n_row
    )
    core_sum = (near.astype(F32) + flip(far, "core").astype(F32)).astype(BF16)

    def halve(total, axis):
        half = total.shape[0] // 2
        return total[:half].astype(F32) + flip(total[half:], axis).astype(F32)

    pair_sum = halve(core_sum, "z1").astype(BF16)
    line_rows = swap_parts(copies_of(after(line_sum, pair_sum), Z4), Z4).reshape(-1, width)
    quad_sum = halve(pair_sum, "zb").astype(BF16)
    line_rows = after(line_rows, quad_sum)
    weight_grad = swap_parts(copies_of(line_rows, PLANE), PLANE).reshape(width, width)
    feature_grad = halve(quad_sum, "za")[0] * own_scale[:, None]
    return (output, weight_grad, feature_grad)


def solution(mesh):
    fine = Mesh(mesh.devices.reshape(2, 2, 2, 2, 4, 2, 4), AXES)
    nodes, row, col = P(AXES, None), ROW, ("y", "zh", "x")
    in_specs = (
        nodes,
        P(),
        nodes,
        P(row, col, None),
        P(row, col, None),
        P(row, col),
        P(row, col, None, None, None),
    )
    out_specs = (nodes, P(), nodes)
    return jax.shard_map(local, mesh=fine, in_specs=in_specs, out_specs=out_specs, check_vma=False)
```

```python
import functools
import math

import jax
import jax.numpy as jnp
from jax import lax
from jax.experimental import pallas as pl
from jax.experimental.pallas import tpu as pltpu
from jax.sharding import Mesh
from jax.sharding import PartitionSpec as P

AXES = ("za", "zb", "z1", "core", "y", "zh", "x")
Z4 = ("za", "zb")
ROW = ("za", "zb", "z1", "core")
PLANE = ("y", "x")
BF16 = jnp.bfloat16
F32 = jnp.float32


def layer_rows(row_total, grad_rows, weight):
    inv_rms = lax.rsqrt(jnp.mean(row_total * row_total, axis=1, keepdims=True) + 1e-06)
    norm_f32 = row_total * inv_rms
    normed = norm_f32.astype(BF16)
    pre_act = jnp.dot(normed, weight, preferred_element_type=F32)
    output = jax.nn.silu(pre_act).astype(BF16)
    sigmoid_pre = jax.nn.sigmoid(pre_act)
    act_slope = sigmoid_pre * (1.0 + pre_act * (1.0 - sigmoid_pre))
    grad_pre = (grad_rows.astype(F32) * act_slope).astype(BF16)
    grad_norm = jnp.einsum("ng,fg->nf", grad_pre, weight, preferred_element_type=F32)
    grad_z = (
        inv_rms * (grad_norm - norm_f32 * jnp.mean(grad_norm * norm_f32, axis=1, keepdims=True))
    ).astype(BF16)
    return (output, normed, grad_pre, grad_z)


def flip(block, axis):
    return lax.ppermute(block, axis, [(0, 1), (1, 0)])


def after(value, *others):
    return lax.optimization_barrier((value,) + others)[0]


def swap_parts(parts, axes):
    return lax.all_to_all(parts, axes, split_axis=0, concat_axis=0, tiled=True)


def copies_of(block, axes):
    return jnp.broadcast_to(block[None], (lax.axis_size(axes),) + block.shape)


def tile_kernel(transposed, scaled, sources, places, source, target, count, tiles, *refs):
    scale, refs = (refs[0], refs[1:]) if scaled else (None, refs)
    total = refs[-1]
    arrays, outputs = refs[: -1 - len(places)], refs[-1 - len(places) : -1]
    slots, size, _ = tiles.shape
    axis = 0 if transposed else 1
    total[...] = jnp.zeros_like(total)
    for slot in range(slots):

        def add(block):
            if scaled:
                row = jnp.broadcast_to(scale[slot : slot + 1, :], (size, size))
                column = jnp.transpose(row)
                lanes = [block[:, i : i + size] for i in range(0, block.shape[1], size)]
                lanes = [(part.astype(F32) * column).astype(BF16) for part in lanes]
                block = jnp.concatenate(lanes, axis=1)
            total[target[slot]] += lax.dot_general(
                tiles[slot], block, (((axis,), (0,)), ((), ())), preferred_element_type=F32
            )

        first = 0
        for pieces in sources:
            held = arrays[pieces[0][0]].shape[0]
            inside = source[slot] - first
            first += held

            @pl.when((slot < count[0]) & (inside >= 0) & (inside < held))
            def _(pieces=pieces, inside=jnp.clip(inside, 0, held - 1)):
                rows = [arrays[number][inside, low:high, :] for number, low, high in pieces]
                add(rows[0] if len(rows) == 1 else jnp.concatenate(rows, axis=0))

    for output, pieces in zip(outputs, places):
        row = 0
        for start, stop, low, high in pieces:
            output[:, row : row + high - low, :] = total[start:stop, low:high, :].astype(BF16)
            row += high - low


def tile_sums(transposed, source, target, count, tiles, scale, arrays, sources, places, blocks):
    slots, size, _ = tiles.shape
    width = arrays[0].shape[2]
    smem = pl.BlockSpec(memory_space=pltpu.SMEM)
    vmem = pl.BlockSpec(memory_space=pltpu.VMEM)
    scaled = scale is not None
    operands = [tiles] + [scale] * scaled + list(arrays)
    shapes = [
        (pieces[0][1] - pieces[0][0], sum(high - low for _, _, low, high in pieces), width)
        for pieces in places
    ]
    return pl.pallas_call(
        functools.partial(tile_kernel, transposed, scaled, sources, places),
        out_shape=[jax.ShapeDtypeStruct(shape, BF16) for shape in shapes],
        in_specs=[smem] * 3 + [vmem] * len(operands),
        out_specs=[vmem] * len(shapes),
        scratch_shapes=[pltpu.VMEM((blocks, size, width), F32)],
        compiler_params=pltpu.CompilerParams(vmem_limit_bytes=40 * 1024 * 1024),
        cost_estimate=pl.CostEstimate(
            flops=2 * slots * size * size * width,
            bytes_accessed=6 * blocks * size * width,
            transcendentals=0,
        ),
    )(source, target, count, *operands)


def local(features, weight, cotangent, tile_rows, tile_cols, tile_count, tile_vals):
    span, width = features.shape
    n_z4, n_z1, n_core = lax.axis_size(Z4), lax.axis_size("z1"), lax.axis_size("core")
    n_y, n_zh, n_x = lax.axis_size("y"), lax.axis_size("zh"), lax.axis_size("x")
    n_line = n_z4 * n_z1
    n_row, n_col = n_line * n_core, n_y * n_zh * n_x
    n_plane = n_y * n_x
    my_row = lax.axis_index(ROW)
    my_zh = lax.axis_index("zh")
    slots = tile_vals.shape[2]
    nodes = n_row * n_col * span
    tiles = tile_vals[0, 0]
    count = tile_count[0]
    row_index = tile_rows[0, 0]
    col_index = tile_cols[0, 0]
    col_bits = col_index ^ my_row
    col_near = (col_bits & 1) * n_line + (col_bits & 2) * (n_z4 // 2)
    col_from = col_near + (col_index >> 2)
    col_to = col_near + ((col_bits >> 2) & 1) * 2 + (col_bits >> 3)
    row_plane = (row_index >> 3) * n_x + (row_index & 3)
    row_place = (((row_index >> 2) & 1) ^ my_zh) * n_plane + row_plane

    alive = (jnp.arange(slots, dtype=jnp.int32) < count[0]).astype(F32)
    order_cols = (col_index[:, None] == jnp.arange(n_row, dtype=jnp.int32)[None, :]).astype(F32)
    col_sums = jnp.sum(tiles, axis=1, dtype=F32) * alive[:, None]
    degree_terms = jnp.einsum("sc,sj->cj", order_cols, col_sums, precision=lax.Precision.HIGHEST)
    high = lax.reduce_precision(degree_terms, 8, 7)
    pieces = jnp.stack([high, degree_terms - high]).astype(BF16).reshape(-1, width)
    own_line = swap_parts(copies_of(jnp.concatenate([features, pieces]), Z4), Z4)
    own_pair = flip(own_line, "z1")
    blocks = [own_line, own_pair, flip(own_line, "core"), flip(own_pair, "core")]

    def degrees(part):
        return jnp.sum(part[:, span:].astype(F32).reshape(-1, n_row, span), axis=0)

    col_scale = lax.rsqrt(1.0 + sum(degrees(part) for part in blocks))
    own_scale = lax.dynamic_index_in_dim(col_scale, my_row, axis=0, keepdims=False)
    slot_scale = col_scale[col_index]

    half = span // 2
    first_terms, last_terms = tile_sums(
        False,
        col_from,
        row_place,
        count,
        tiles,
        slot_scale,
        blocks,
        [[(number, 0, span)] for number in range(4)],
        [[(n_plane, n_col, 0, span), (0, n_plane, 0, half)], [(0, n_plane, half, span)]],
        n_col,
    )
    first_group = swap_parts(first_terms, PLANE)
    far_sum = jnp.sum(first_group[:, :span].astype(F32), axis=0).astype(BF16)
    last_group = swap_parts(after(last_terms, far_sum), PLANE)
    near_sum = jnp.concatenate(
        [
            jnp.sum(first_group[:, span:].astype(F32), axis=0),
            jnp.sum(last_group.astype(F32), axis=0),
        ]
    )
    own_total = near_sum + flip(far_sum, "zh").astype(F32)

    output, normed, grad_pre, grad_own = layer_rows(own_total, cotangent, weight)

    weight_terms = jnp.einsum("nf,ng->fg", normed, grad_pre, preferred_element_type=F32)
    weight_parts = weight_terms.astype(BF16).reshape(n_plane, width // n_plane, width)
    first_group = swap_parts(
        jnp.concatenate([copies_of(grad_own[:half], PLANE), weight_parts], axis=1), PLANE
    )
    grad_rest = jnp.concatenate([grad_own[half:], flip(grad_own, "zh")])
    last_group = swap_parts(copies_of(after(grad_rest, first_group), PLANE), PLANE)

    line_rows = jnp.sum(first_group[:, half:].astype(F32), axis=0)
    for axis in ("core", "z1", "zb", "za", "zh"):
        line_rows = line_rows + flip(line_rows, axis)
    line_rows = line_rows * (1.0 / math.sqrt(nodes))
    last_group = after(last_group, line_rows)

    near, far = tile_sums(
        True,
        row_place,
        col_to,
        count,
        tiles,
        None,
        [first_group, last_group],
        [[(0, 0, half), (1, 0, half)], [(1, half, half + span)]],
        [[(0, n_line, 0, span)], [(n_line, n_row, 0, span)]],
        n_row,
    )
    core_sum = (near.astype(F32) + flip(far, "core").astype(F32)).astype(BF16)

    def halve(total, axis):
        half = total.shape[0] // 2
        return total[:half].astype(F32) + flip(total[half:], axis).astype(F32)

    line_rows = after(line_rows, core_sum)
    weight_grad = swap_parts(copies_of(line_rows, PLANE), PLANE).reshape(width, width)
    pair_sum = halve(core_sum, "z1").astype(BF16)
    quad_sum = halve(pair_sum, "zb").astype(BF16)
    feature_grad = halve(quad_sum, "za")[0] * own_scale[:, None]
    return (output, weight_grad, feature_grad)


def solution(mesh):
    fine = Mesh(mesh.devices.reshape(2, 2, 2, 2, 4, 2, 4), AXES)
    nodes, row, col = P(AXES, None), ROW, ("y", "zh", "x")
    in_specs = (
        nodes,
        P(),
        nodes,
        P(row, col, None),
        P(row, col, None),
        P(row, col),
        P(row, col, None, None, None),
    )
    out_specs = (nodes, P(), nodes)
    return jax.shard_map(local, mesh=fine, in_specs=in_specs, out_specs=out_specs, check_vma=False)
```

```python
import functools
import math

import jax
import jax.numpy as jnp
from jax import lax
from jax.experimental import pallas as pl
from jax.experimental.pallas import tpu as pltpu
from jax.sharding import Mesh
from jax.sharding import PartitionSpec as P

AXES = ("za", "zb", "z1", "core", "y", "zh", "x")
Z4 = ("za", "zb")
ROW = ("za", "zb", "z1", "core")
PLANE = ("y", "x")
BF16 = jnp.bfloat16
F32 = jnp.float32


def layer_rows(row_total, grad_rows, weight):
    inv_rms = lax.rsqrt(jnp.mean(row_total * row_total, axis=1, keepdims=True) + 1e-06)
    norm_f32 = row_total * inv_rms
    normed = norm_f32.astype(BF16)
    pre_act = jnp.dot(normed, weight, preferred_element_type=F32)
    output = jax.nn.silu(pre_act).astype(BF16)
    sigmoid_pre = jax.nn.sigmoid(pre_act)
    act_slope = sigmoid_pre * (1.0 + pre_act * (1.0 - sigmoid_pre))
    grad_pre = (grad_rows.astype(F32) * act_slope).astype(BF16)
    grad_norm = jnp.einsum("ng,fg->nf", grad_pre, weight, preferred_element_type=F32)
    grad_z = (
        inv_rms * (grad_norm - norm_f32 * jnp.mean(grad_norm * norm_f32, axis=1, keepdims=True))
    ).astype(BF16)
    return (output, normed, grad_pre, grad_z)


def flip(block, axis):
    return lax.ppermute(block, axis, [(0, 1), (1, 0)])


def after(value, *others):
    return lax.optimization_barrier((value,) + others)[0]


def swap_parts(parts, axes):
    return lax.all_to_all(parts, axes, split_axis=0, concat_axis=0, tiled=True)


def copies_of(block, axes):
    return jnp.broadcast_to(block[None], (lax.axis_size(axes),) + block.shape)


def tile_kernel(transposed, scaled, sources, places, source, target, count, tiles, *refs):
    scale, refs = (refs[0], refs[1:]) if scaled else (None, refs)
    total = refs[-1]
    arrays, outputs = refs[: -1 - len(places)], refs[-1 - len(places) : -1]
    slots, size, _ = tiles.shape
    axis = 0 if transposed else 1
    total[...] = jnp.zeros_like(total)
    for slot in range(slots):

        def add(block):
            if scaled:
                row = jnp.broadcast_to(scale[slot : slot + 1, :], (size, size))
                column = jnp.transpose(row)
                lanes = [block[:, i : i + size] for i in range(0, block.shape[1], size)]
                lanes = [(part.astype(F32) * column).astype(BF16) for part in lanes]
                block = jnp.concatenate(lanes, axis=1)
            total[target[slot]] += lax.dot_general(
                tiles[slot], block, (((axis,), (0,)), ((), ())), preferred_element_type=F32
            )

        first = 0
        for pieces in sources:
            held = arrays[pieces[0][0]].shape[0]
            inside = source[slot] - first
            first += held

            @pl.when((slot < count[0]) & (inside >= 0) & (inside < held))
            def _(pieces=pieces, inside=jnp.clip(inside, 0, held - 1)):
                rows = [arrays[number][inside, low:high, :] for number, low, high in pieces]
                add(rows[0] if len(rows) == 1 else jnp.concatenate(rows, axis=0))

    for output, pieces in zip(outputs, places):
        row = 0
        for start, stop, low, high in pieces:
            output[:, row : row + high - low, :] = total[start:stop, low:high, :].astype(BF16)
            row += high - low


def tile_sums(transposed, source, target, count, tiles, scale, arrays, sources, places, blocks):
    slots, size, _ = tiles.shape
    width = arrays[0].shape[2]
    smem = pl.BlockSpec(memory_space=pltpu.SMEM)
    vmem = pl.BlockSpec(memory_space=pltpu.VMEM)
    scaled = scale is not None
    operands = [tiles] + [scale] * scaled + list(arrays)
    shapes = [
        (pieces[0][1] - pieces[0][0], sum(high - low for _, _, low, high in pieces), width)
        for pieces in places
    ]
    return pl.pallas_call(
        functools.partial(tile_kernel, transposed, scaled, sources, places),
        out_shape=[jax.ShapeDtypeStruct(shape, BF16) for shape in shapes],
        in_specs=[smem] * 3 + [vmem] * len(operands),
        out_specs=[vmem] * len(shapes),
        scratch_shapes=[pltpu.VMEM((blocks, size, width), F32)],
        compiler_params=pltpu.CompilerParams(vmem_limit_bytes=40 * 1024 * 1024),
        cost_estimate=pl.CostEstimate(
            flops=2 * slots * size * size * width,
            bytes_accessed=6 * blocks * size * width,
            transcendentals=0,
        ),
    )(source, target, count, *operands)


def local(features, weight, cotangent, tile_rows, tile_cols, tile_count, tile_vals):
    span, width = features.shape
    n_z4, n_z1, n_core = lax.axis_size(Z4), lax.axis_size("z1"), lax.axis_size("core")
    n_y, n_zh, n_x = lax.axis_size("y"), lax.axis_size("zh"), lax.axis_size("x")
    n_line = n_z4 * n_z1
    n_row, n_col = n_line * n_core, n_y * n_zh * n_x
    n_plane = n_y * n_x
    my_row = lax.axis_index(ROW)
    my_zh = lax.axis_index("zh")
    slots = tile_vals.shape[2]
    nodes = n_row * n_col * span
    tiles = tile_vals[0, 0]
    count = tile_count[0]
    row_index = tile_rows[0, 0]
    col_index = tile_cols[0, 0]
    col_bits = col_index ^ my_row
    col_near = (col_bits & 1) * n_line + (col_bits & 2) * (n_z4 // 2)
    col_from = col_near + (col_index >> 2)
    col_to = col_near + ((col_bits >> 2) & 1) * 2 + (col_bits >> 3)
    row_plane = (row_index >> 3) * n_x + (row_index & 3)
    row_place = (((row_index >> 2) & 1) ^ my_zh) * n_plane + row_plane

    alive = (jnp.arange(slots, dtype=jnp.int32) < count[0]).astype(F32)
    order_cols = (col_index[:, None] == jnp.arange(n_row, dtype=jnp.int32)[None, :]).astype(F32)
    col_sums = jnp.sum(tiles, axis=1, dtype=F32) * alive[:, None]
    degree_terms = jnp.einsum("sc,sj->cj", order_cols, col_sums, precision=lax.Precision.HIGHEST)
    high = lax.reduce_precision(degree_terms, 8, 7)
    pieces = jnp.stack([high, degree_terms - high]).astype(BF16).reshape(-1, width)
    own_line = swap_parts(copies_of(jnp.concatenate([features, pieces]), Z4), Z4)
    own_pair = flip(own_line, "z1")
    blocks = [own_line, own_pair, flip(own_line, "core"), flip(own_pair, "core")]

    def degrees(part):
        return jnp.sum(part[:, span:].astype(F32).reshape(-1, n_row, span), axis=0)

    col_scale = lax.rsqrt(1.0 + sum(degrees(part) for part in blocks))
    own_scale = lax.dynamic_index_in_dim(col_scale, my_row, axis=0, keepdims=False)
    slot_scale = col_scale[col_index]

    near_terms, far_terms = tile_sums(
        False,
        col_from,
        row_place,
        count,
        tiles,
        slot_scale,
        blocks,
        [[(number, 0, span)] for number in range(4)],
        [[(0, n_plane, 0, span)], [(n_plane, n_col, 0, span)]],
        n_col,
    )
    far_sum = jnp.sum(swap_parts(far_terms, PLANE).astype(F32), axis=0).astype(BF16)
    near_group = swap_parts(after(near_terms, far_sum), PLANE)
    own_total = jnp.sum(near_group.astype(F32), axis=0) + flip(far_sum, "zh").astype(F32)

    output, normed, grad_pre, grad_own = layer_rows(own_total, cotangent, weight)

    weight_terms = jnp.einsum("nf,ng->fg", normed, grad_pre, preferred_element_type=F32)
    weight_parts = weight_terms.astype(BF16).reshape(n_plane, width // n_plane, width)
    near_group = swap_parts(
        jnp.concatenate([copies_of(grad_own, PLANE), weight_parts], axis=1), PLANE
    )
    far_group = swap_parts(copies_of(after(flip(grad_own, "zh"), near_group), PLANE), PLANE)

    line_rows = jnp.sum(near_group[:, span:].astype(F32), axis=0)
    for axis in ("core", "z1", "zb", "zh"):
        line_rows = line_rows + flip(line_rows, axis)
    line_rows = line_rows * (1.0 / math.sqrt(nodes))
    far_group = after(far_group, line_rows)

    near, far = tile_sums(
        True,
        row_place,
        col_to,
        count,
        tiles,
        None,
        [near_group, far_group],
        [[(0, 0, span)], [(1, 0, span)]],
        [[(0, n_line, 0, span)], [(n_line, n_row, 0, span)]],
        n_row,
    )
    core_sum = (near.astype(F32) + flip(far, "core").astype(F32)).astype(BF16)

    def halve(total, axis):
        half = total.shape[0] // 2
        return total[:half].astype(F32) + flip(total[half:], axis).astype(F32)

    line_rows = after(line_rows, core_sum)
    line_rows = line_rows + flip(line_rows, "za")
    pair_sum = halve(core_sum, "z1").astype(BF16)
    weight_grad = swap_parts(copies_of(line_rows, PLANE), PLANE).reshape(width, width)
    quad_sum = halve(pair_sum, "zb").astype(BF16)
    feature_grad = halve(quad_sum, "za")[0] * own_scale[:, None]
    return (output, weight_grad, feature_grad)


def solution(mesh):
    fine = Mesh(mesh.devices.reshape(2, 2, 2, 2, 4, 2, 4), AXES)
    nodes, row, col = P(AXES, None), ROW, ("y", "zh", "x")
    in_specs = (
        nodes,
        P(),
        nodes,
        P(row, col, None),
        P(row, col, None),
        P(row, col),
        P(row, col, None, None, None),
    )
    out_specs = (nodes, P(), nodes)
    return jax.shard_map(local, mesh=fine, in_specs=in_specs, out_specs=out_specs, check_vma=False)
```

```python
import functools
import math

import jax
import jax.numpy as jnp
from jax import lax
from jax.experimental import pallas as pl
from jax.experimental.pallas import tpu as pltpu
from jax.sharding import Mesh
from jax.sharding import PartitionSpec as P

AXES = ("za", "zb", "z1", "core", "y", "zh", "x")
Z4 = ("za", "zb")
ROW = ("za", "zb", "z1", "core")
PLANE = ("y", "x")
CHUNKS = 2
BF16 = jnp.bfloat16
F32 = jnp.float32


def layer_rows(row_total, grad_rows, weight):
    inv_rms = lax.rsqrt(jnp.mean(row_total * row_total, axis=1, keepdims=True) + 1e-06)
    norm_f32 = row_total * inv_rms
    normed = norm_f32.astype(BF16)
    pre_act = jnp.dot(normed, weight, preferred_element_type=F32)
    output = jax.nn.silu(pre_act).astype(BF16)
    sigmoid_pre = jax.nn.sigmoid(pre_act)
    act_slope = sigmoid_pre * (1.0 + pre_act * (1.0 - sigmoid_pre))
    grad_pre = (grad_rows.astype(F32) * act_slope).astype(BF16)
    grad_norm = jnp.einsum("ng,fg->nf", grad_pre, weight, preferred_element_type=F32)
    grad_z = (
        inv_rms * (grad_norm - norm_f32 * jnp.mean(grad_norm * norm_f32, axis=1, keepdims=True))
    ).astype(BF16)
    return (output, normed, grad_pre, grad_z)


def flip(block, axis):
    return lax.ppermute(block, axis, [(0, 1), (1, 0)])


def after(value, *others):
    return lax.optimization_barrier((value,) + others)[0]


def swap_parts(parts, axes):
    return lax.all_to_all(parts, axes, split_axis=0, concat_axis=0, tiled=True)


def copies_of(block, axes):
    return jnp.broadcast_to(block[None], (lax.axis_size(axes),) + block.shape)


def tile_kernel(transposed, scaled, sources, places, source, target, count, tiles, *refs):
    scale, refs = (refs[0], refs[1:]) if scaled else (None, refs)
    total = refs[-1]
    arrays, outputs = refs[: -1 - len(places)], refs[-1 - len(places) : -1]
    slots, size, _ = tiles.shape
    axis = 0 if transposed else 1
    total[...] = jnp.zeros_like(total)
    for slot in range(slots):

        def add(block, left):
            if scaled:
                row = jnp.broadcast_to(scale[slot : slot + 1, :], (size, size))
                column = jnp.transpose(row)
                lanes = [block[:, i : i + size] for i in range(0, block.shape[1], size)]
                lanes = [(part.astype(F32) * column).astype(BF16) for part in lanes]
                block = jnp.concatenate(lanes, axis=1)
            total[target[slot], :, left : left + block.shape[1]] += lax.dot_general(
                tiles[slot], block, (((axis,), (0,)), ((), ())), preferred_element_type=F32
            )

        first = 0
        for chunks in sources:
            held = arrays[chunks[0][0][0]].shape[0]
            inside = source[slot] - first
            first += held

            @pl.when((slot < count[0]) & (inside >= 0) & (inside < held))
            def _(chunks=chunks, inside=jnp.clip(inside, 0, held - 1)):
                left = 0
                for pieces in chunks:
                    rows = [arrays[number][inside, low:high, :] for number, low, high in pieces]
                    block = rows[0] if len(rows) == 1 else jnp.concatenate(rows, axis=0)
                    add(block, left)
                    left += block.shape[1]

    for output, (left, right, pieces) in zip(outputs, places):
        row = 0
        for start, stop, low, high in pieces:
            part = total[start:stop, low:high, left:right]
            output[:, row : row + high - low, :] = part.astype(BF16)
            row += high - low


def tile_sums(transposed, source, target, count, tiles, scale, arrays, sources, places, blocks):
    slots, size, _ = tiles.shape
    width = sum(arrays[pieces[0][0]].shape[2] for pieces in sources[0])
    smem = pl.BlockSpec(memory_space=pltpu.SMEM)
    vmem = pl.BlockSpec(memory_space=pltpu.VMEM)
    scaled = scale is not None
    operands = [tiles] + [scale] * scaled + list(arrays)
    shapes = [
        (pieces[0][1] - pieces[0][0], sum(high - low for _, _, low, high in pieces), right - left)
        for left, right, pieces in places
    ]
    return pl.pallas_call(
        functools.partial(tile_kernel, transposed, scaled, sources, places),
        out_shape=[jax.ShapeDtypeStruct(shape, BF16) for shape in shapes],
        in_specs=[smem] * 3 + [vmem] * len(operands),
        out_specs=[vmem] * len(shapes),
        scratch_shapes=[pltpu.VMEM((blocks, size, width), F32)],
        compiler_params=pltpu.CompilerParams(vmem_limit_bytes=40 * 1024 * 1024),
        cost_estimate=pl.CostEstimate(
            flops=2 * slots * size * size * width,
            bytes_accessed=6 * blocks * size * width,
            transcendentals=0,
        ),
    )(source, target, count, *operands)


def local(features, weight, cotangent, tile_rows, tile_cols, tile_count, tile_vals):
    span, width = features.shape
    n_z4, n_z1, n_core = lax.axis_size(Z4), lax.axis_size("z1"), lax.axis_size("core")
    n_y, n_zh, n_x = lax.axis_size("y"), lax.axis_size("zh"), lax.axis_size("x")
    n_line = n_z4 * n_z1
    n_row, n_col = n_line * n_core, n_y * n_zh * n_x
    n_plane = n_y * n_x
    my_row = lax.axis_index(ROW)
    my_zh = lax.axis_index("zh")
    slots = tile_vals.shape[2]
    nodes = n_row * n_col * span
    tiles = tile_vals[0, 0]
    count = tile_count[0]
    row_index = tile_rows[0, 0]
    col_index = tile_cols[0, 0]
    col_bits = col_index ^ my_row
    col_place = (col_bits & 1) * n_line + (col_bits & 2) * (n_z4 // 2)
    col_place = col_place + ((col_bits >> 2) & 1) * 2 + (col_bits >> 3)
    row_plane = (row_index >> 3) * n_x + (row_index & 3)
    row_place = (((row_index >> 2) & 1) ^ my_zh) * n_plane + row_plane

    alive = (jnp.arange(slots, dtype=jnp.int32) < count[0]).astype(F32)
    order_cols = (col_index[:, None] == jnp.arange(n_row, dtype=jnp.int32)[None, :]).astype(F32)
    col_sums = jnp.sum(tiles, axis=1, dtype=F32) * alive[:, None]
    degree_terms = jnp.einsum("sc,sj->cj", order_cols, col_sums, precision=lax.Precision.HIGHEST)
    high = lax.reduce_precision(degree_terms, 8, 7)
    pieces = jnp.stack([high, degree_terms - high]).astype(BF16)
    chunk = width // CHUNKS
    parts = [slice(c * chunk, (c + 1) * chunk) for c in range(CHUNKS)]
    held = [features[None, :, part] for part in parts]
    held[0] = jnp.concatenate([held[0], pieces.reshape(1, -1, chunk)], axis=1)
    for axis in Z4:
        held = [jnp.concatenate([part, flip(part, axis)]) for part in held]
    pairs = [flip(part, "z1") for part in held]
    groups = [held, pairs] + [[flip(part, "core") for part in group] for group in (held, pairs)]

    def degrees(part):
        return jnp.sum(part[:, span:].astype(F32).reshape(-1, n_row, span), axis=0)

    col_scale = lax.rsqrt(1.0 + sum(degrees(group[0]) for group in groups))
    own_scale = lax.dynamic_index_in_dim(col_scale, my_row, axis=0, keepdims=False)
    slot_scale = col_scale[col_index]

    near_terms, far_terms = tile_sums(
        False,
        col_place,
        row_place,
        count,
        tiles,
        slot_scale,
        sum(groups, []),
        [[[(g * CHUNKS + c, 0, span)] for c in range(CHUNKS)] for g in range(len(groups))],
        [(0, width, [(0, n_plane, 0, span)]), (0, width, [(n_plane, n_col, 0, span)])],
        n_col,
    )
    far_sum = jnp.sum(swap_parts(far_terms, PLANE).astype(F32), axis=0).astype(BF16)
    near_group = swap_parts(after(near_terms, far_sum), PLANE)
    own_total = jnp.sum(near_group.astype(F32), axis=0) + flip(far_sum, "zh").astype(F32)

    output, normed, grad_pre, grad_own = layer_rows(own_total, cotangent, weight)

    half = span // 2
    weight_terms = jnp.einsum("nf,ng->fg", normed, grad_pre, preferred_element_type=F32)
    weight_parts = weight_terms.astype(BF16).reshape(n_plane, width // n_plane, width)
    first_group = swap_parts(
        jnp.concatenate([copies_of(grad_own[:half], PLANE), weight_parts], axis=1), PLANE
    )
    grad_rest = jnp.concatenate([grad_own[half:], flip(grad_own, "zh")])
    last_group = swap_parts(copies_of(after(grad_rest, first_group), PLANE), PLANE)

    line_rows = jnp.sum(first_group[:, half:].astype(F32), axis=0)
    for axis in ("core", "z1", "zb", "za", "zh"):
        line_rows = line_rows + flip(line_rows, axis)
    line_rows = line_rows * (1.0 / math.sqrt(nodes))
    last_group = after(last_group, line_rows)

    halves = tile_sums(
        True,
        row_place,
        col_place,
        count,
        tiles,
        None,
        [first_group, last_group],
        [[[(0, 0, half), (1, 0, half)]], [[(1, half, half + span)]]],
        [
            (part.start, part.stop, [(first, first + n_line, 0, span)])
            for first in (0, n_line)
            for part in parts
        ],
        n_row,
    )
    totals = [
        keep.astype(F32) + flip(send, "core").astype(F32)
        for keep, send in zip(halves[:CHUNKS], halves[CHUNKS:])
    ]
    line_rows = after(line_rows, *totals)
    weight_grad = swap_parts(copies_of(line_rows, PLANE), PLANE).reshape(width, width)
    for axis in ("z1", "zb", "za"):
        totals = [total.astype(BF16) for total in totals]
        size = totals[0].shape[0] // 2
        totals = [
            total[:size].astype(F32) + flip(total[size:], axis).astype(F32) for total in totals
        ]
    feature_grad = jnp.concatenate([total[0] for total in totals], axis=1) * own_scale[:, None]
    return (output, weight_grad, feature_grad)


def solution(mesh):
    fine = Mesh(mesh.devices.reshape(2, 2, 2, 2, 4, 2, 4), AXES)
    nodes, row, col = P(AXES, None), ROW, ("y", "zh", "x")
    in_specs = (
        nodes,
        P(),
        nodes,
        P(row, col, None),
        P(row, col, None),
        P(row, col),
        P(row, col, None, None, None),
    )
    out_specs = (nodes, P(), nodes)
    return jax.shard_map(local, mesh=fine, in_specs=in_specs, out_specs=out_specs, check_vma=False)
```

```python
import functools
import math

import jax
import jax.numpy as jnp
from jax import lax
from jax.experimental import pallas as pl
from jax.experimental.pallas import tpu as pltpu
from jax.sharding import Mesh
from jax.sharding import PartitionSpec as P

AXES = ("za", "zb", "z1", "core", "y", "zh", "x")
Z4 = ("za", "zb")
ROW = ("za", "zb", "z1", "core")
PLANE = ("y", "x")
CHUNKS = 2
BF16 = jnp.bfloat16
F32 = jnp.float32


def layer_rows(row_total, grad_rows, weight):
    inv_rms = lax.rsqrt(jnp.mean(row_total * row_total, axis=1, keepdims=True) + 1e-06)
    norm_f32 = row_total * inv_rms
    normed = norm_f32.astype(BF16)
    pre_act = jnp.dot(normed, weight, preferred_element_type=F32)
    output = jax.nn.silu(pre_act).astype(BF16)
    sigmoid_pre = jax.nn.sigmoid(pre_act)
    act_slope = sigmoid_pre * (1.0 + pre_act * (1.0 - sigmoid_pre))
    grad_pre = (grad_rows.astype(F32) * act_slope).astype(BF16)
    grad_norm = jnp.einsum("ng,fg->nf", grad_pre, weight, preferred_element_type=F32)
    grad_z = (
        inv_rms * (grad_norm - norm_f32 * jnp.mean(grad_norm * norm_f32, axis=1, keepdims=True))
    ).astype(BF16)
    return (output, normed, grad_pre, grad_z)


def flip(block, axis):
    return lax.ppermute(block, axis, [(0, 1), (1, 0)])


def after(value, *others):
    return lax.optimization_barrier((value,) + others)[0]


def swap_parts(parts, axes):
    return lax.all_to_all(parts, axes, split_axis=0, concat_axis=0, tiled=True)


def copies_of(block, axes):
    return jnp.broadcast_to(block[None], (lax.axis_size(axes),) + block.shape)


def tile_kernel(transposed, scaled, sources, places, source, target, count, tiles, *refs):
    scale, refs = (refs[0], refs[1:]) if scaled else (None, refs)
    total = refs[-1]
    arrays, outputs = refs[: -1 - len(places)], refs[-1 - len(places) : -1]
    slots, size, _ = tiles.shape
    axis = 0 if transposed else 1
    total[...] = jnp.zeros_like(total)
    for slot in range(slots):

        def add(block, left):
            if scaled:
                row = jnp.broadcast_to(scale[slot : slot + 1, :], (size, size))
                column = jnp.transpose(row)
                lanes = [block[:, i : i + size] for i in range(0, block.shape[1], size)]
                lanes = [(part.astype(F32) * column).astype(BF16) for part in lanes]
                block = jnp.concatenate(lanes, axis=1)
            total[target[slot], :, left : left + block.shape[1]] += lax.dot_general(
                tiles[slot], block, (((axis,), (0,)), ((), ())), preferred_element_type=F32
            )

        first = 0
        for chunks in sources:
            held = arrays[chunks[0][0][0]].shape[0]
            inside = source[slot] - first
            first += held

            @pl.when((slot < count[0]) & (inside >= 0) & (inside < held))
            def _(chunks=chunks, inside=jnp.clip(inside, 0, held - 1)):
                left = 0
                for pieces in chunks:
                    rows = [arrays[number][inside, low:high, :] for number, low, high in pieces]
                    block = rows[0] if len(rows) == 1 else jnp.concatenate(rows, axis=0)
                    add(block, left)
                    left += block.shape[1]

    for output, (left, right, pieces) in zip(outputs, places):
        row = 0
        for start, stop, low, high in pieces:
            part = total[start:stop, low:high, left:right]
            output[:, row : row + high - low, :] = part.astype(BF16)
            row += high - low


def tile_sums(transposed, source, target, count, tiles, scale, arrays, sources, places, blocks):
    slots, size, _ = tiles.shape
    width = sum(arrays[pieces[0][0]].shape[2] for pieces in sources[0])
    smem = pl.BlockSpec(memory_space=pltpu.SMEM)
    vmem = pl.BlockSpec(memory_space=pltpu.VMEM)
    scaled = scale is not None
    operands = [tiles] + [scale] * scaled + list(arrays)
    shapes = [
        (pieces[0][1] - pieces[0][0], sum(high - low for _, _, low, high in pieces), right - left)
        for left, right, pieces in places
    ]
    return pl.pallas_call(
        functools.partial(tile_kernel, transposed, scaled, sources, places),
        out_shape=[jax.ShapeDtypeStruct(shape, BF16) for shape in shapes],
        in_specs=[smem] * 3 + [vmem] * len(operands),
        out_specs=[vmem] * len(shapes),
        scratch_shapes=[pltpu.VMEM((blocks, size, width), F32)],
        compiler_params=pltpu.CompilerParams(vmem_limit_bytes=40 * 1024 * 1024),
        cost_estimate=pl.CostEstimate(
            flops=2 * slots * size * size * width,
            bytes_accessed=6 * blocks * size * width,
            transcendentals=0,
        ),
    )(source, target, count, *operands)


def local(features, weight, cotangent, tile_rows, tile_cols, tile_count, tile_vals):
    span, width = features.shape
    n_z4, n_z1, n_core = lax.axis_size(Z4), lax.axis_size("z1"), lax.axis_size("core")
    n_y, n_zh, n_x = lax.axis_size("y"), lax.axis_size("zh"), lax.axis_size("x")
    n_line = n_z4 * n_z1
    n_row, n_col = n_line * n_core, n_y * n_zh * n_x
    n_plane = n_y * n_x
    my_row = lax.axis_index(ROW)
    my_zh = lax.axis_index("zh")
    slots = tile_vals.shape[2]
    nodes = n_row * n_col * span
    tiles = tile_vals[0, 0]
    count = tile_count[0]
    row_index = tile_rows[0, 0]
    col_index = tile_cols[0, 0]
    col_bits = col_index ^ my_row
    col_place = (col_bits & 1) * n_line + (col_bits & 2) * (n_z4 // 2)
    col_place = col_place + ((col_bits >> 2) & 1) * 2 + (col_bits >> 3)
    row_plane = (row_index >> 3) * n_x + (row_index & 3)
    row_place = (((row_index >> 2) & 1) ^ my_zh) * n_plane + row_plane

    alive = (jnp.arange(slots, dtype=jnp.int32) < count[0]).astype(F32)
    order_cols = (col_index[:, None] == jnp.arange(n_row, dtype=jnp.int32)[None, :]).astype(F32)
    col_sums = jnp.sum(tiles, axis=1, dtype=F32) * alive[:, None]
    degree_terms = jnp.einsum("sc,sj->cj", order_cols, col_sums, precision=lax.Precision.HIGHEST)
    high = lax.reduce_precision(degree_terms, 8, 7)
    pieces = jnp.stack([high, degree_terms - high]).astype(BF16)
    chunk = width // CHUNKS
    parts = [slice(c * chunk, (c + 1) * chunk) for c in range(CHUNKS)]
    held = [features[None, :, part] for part in parts]
    held[0] = jnp.concatenate([held[0], pieces.reshape(1, -1, chunk)], axis=1)
    for axis in Z4:
        held = [jnp.concatenate([part, flip(part, axis)]) for part in held]
    pairs = [flip(part, "z1") for part in held]
    groups = [held, pairs] + [[flip(part, "core") for part in group] for group in (held, pairs)]

    def degrees(part):
        return jnp.sum(part[:, span:].astype(F32).reshape(-1, n_row, span), axis=0)

    col_scale = lax.rsqrt(1.0 + sum(degrees(group[0]) for group in groups))
    own_scale = lax.dynamic_index_in_dim(col_scale, my_row, axis=0, keepdims=False)
    slot_scale = col_scale[col_index]

    near_terms, far_terms = tile_sums(
        False,
        col_place,
        row_place,
        count,
        tiles,
        slot_scale,
        sum(groups, []),
        [[[(g * CHUNKS + c, 0, span)] for c in range(CHUNKS)] for g in range(len(groups))],
        [(0, width, [(0, n_plane, 0, span)]), (0, width, [(n_plane, n_col, 0, span)])],
        n_col,
    )
    far_sum = jnp.sum(swap_parts(far_terms, PLANE).astype(F32), axis=0).astype(BF16)
    near_group = swap_parts(after(near_terms, far_sum), PLANE)
    own_total = jnp.sum(near_group.astype(F32), axis=0) + flip(far_sum, "zh").astype(F32)

    output, normed, grad_pre, grad_own = layer_rows(own_total, cotangent, weight)

    lead = span // 4
    weight_terms = jnp.einsum("nf,ng->fg", normed, grad_pre, preferred_element_type=F32)
    weight_parts = weight_terms.astype(BF16).reshape(n_plane, width // n_plane, width)
    first_group = swap_parts(
        jnp.concatenate([copies_of(grad_own[:lead], PLANE), weight_parts], axis=1), PLANE
    )
    grad_rest = jnp.concatenate([grad_own[lead:], flip(grad_own, "zh")])
    last_group = swap_parts(copies_of(after(grad_rest, first_group), PLANE), PLANE)

    line_rows = jnp.sum(first_group[:, lead:].astype(F32), axis=0)
    for axis in ("core", "z1", "zb", "za", "zh"):
        line_rows = line_rows + flip(line_rows, axis)
    line_rows = line_rows * (1.0 / math.sqrt(nodes))
    last_group = after(last_group, line_rows)

    halves = tile_sums(
        True,
        row_place,
        col_place,
        count,
        tiles,
        None,
        [first_group, last_group],
        [[[(0, 0, lead), (1, 0, span - lead)]], [[(1, span - lead, 2 * span - lead)]]],
        [
            (part.start, part.stop, [(first, first + n_line, 0, span)])
            for first in (0, n_line)
            for part in parts
        ],
        n_row,
    )
    totals = [
        keep.astype(F32) + flip(send, "core").astype(F32)
        for keep, send in zip(halves[:CHUNKS], halves[CHUNKS:])
    ]
    along = jnp.concatenate([total[0, :8] for total in totals], axis=1)
    weight_rows = swap_parts(copies_of(jnp.concatenate([line_rows, along]), PLANE), PLANE)
    weight_grad = weight_rows[:, : line_rows.shape[0]].reshape(width, width)
    for axis in ("z1", "zb", "za"):
        totals = [total.astype(BF16) for total in totals]
        size = totals[0].shape[0] // 2
        totals = [
            total[:size].astype(F32) + flip(total[size:], axis).astype(F32) for total in totals
        ]
    feature_grad = jnp.concatenate([total[0] for total in totals], axis=1) * own_scale[:, None]
    return (output, weight_grad, feature_grad)


def solution(mesh):
    fine = Mesh(mesh.devices.reshape(2, 2, 2, 2, 4, 2, 4), AXES)
    nodes, row, col = P(AXES, None), ROW, ("y", "zh", "x")
    in_specs = (
        nodes,
        P(),
        nodes,
        P(row, col, None),
        P(row, col, None),
        P(row, col),
        P(row, col, None, None, None),
    )
    out_specs = (nodes, P(), nodes)
    return jax.shard_map(local, mesh=fine, in_specs=in_specs, out_specs=out_specs, check_vma=False)
```

```python
import functools
import math

import jax
import jax.numpy as jnp
from jax import lax
from jax.experimental import pallas as pl
from jax.experimental.pallas import tpu as pltpu
from jax.sharding import Mesh
from jax.sharding import PartitionSpec as P

AXES = ("za", "zb", "z1", "core", "y", "zh", "x")
Z4 = ("za", "zb")
ROW = ("za", "zb", "z1", "core")
PLANE = ("y", "x")
CHUNKS = 2
BF16 = jnp.bfloat16
F32 = jnp.float32


def layer_rows(row_total, grad_rows, weight):
    inv_rms = lax.rsqrt(jnp.mean(row_total * row_total, axis=1, keepdims=True) + 1e-06)
    norm_f32 = row_total * inv_rms
    normed = norm_f32.astype(BF16)
    pre_act = jnp.dot(normed, weight, preferred_element_type=F32)
    output = jax.nn.silu(pre_act).astype(BF16)
    sigmoid_pre = jax.nn.sigmoid(pre_act)
    act_slope = sigmoid_pre * (1.0 + pre_act * (1.0 - sigmoid_pre))
    grad_pre = (grad_rows.astype(F32) * act_slope).astype(BF16)
    grad_norm = jnp.einsum("ng,fg->nf", grad_pre, weight, preferred_element_type=F32)
    grad_z = (
        inv_rms * (grad_norm - norm_f32 * jnp.mean(grad_norm * norm_f32, axis=1, keepdims=True))
    ).astype(BF16)
    return (output, normed, grad_pre, grad_z)


def flip(block, axis):
    return lax.ppermute(block, axis, [(0, 1), (1, 0)])


def after(value, *others):
    return lax.optimization_barrier((value,) + others)[0]


def swap_parts(parts, axes):
    return lax.all_to_all(parts, axes, split_axis=0, concat_axis=0, tiled=True)


def copies_of(block, axes):
    return jnp.broadcast_to(block[None], (lax.axis_size(axes),) + block.shape)


def tile_kernel(transposed, scaled, sources, places, source, target, count, tiles, *refs):
    scale, refs = (refs[0], refs[1:]) if scaled else (None, refs)
    total = refs[-1]
    arrays, outputs = refs[: -1 - len(places)], refs[-1 - len(places) : -1]
    slots, size, _ = tiles.shape
    axis = 0 if transposed else 1
    total[...] = jnp.zeros_like(total)
    for slot in range(slots):

        def add(block, left):
            if scaled:
                row = jnp.broadcast_to(scale[slot : slot + 1, :], (size, size))
                column = jnp.transpose(row)
                lanes = [block[:, i : i + size] for i in range(0, block.shape[1], size)]
                lanes = [(part.astype(F32) * column).astype(BF16) for part in lanes]
                block = jnp.concatenate(lanes, axis=1)
            total[target[slot], :, left : left + block.shape[1]] += lax.dot_general(
                tiles[slot], block, (((axis,), (0,)), ((), ())), preferred_element_type=F32
            )

        first = 0
        for chunks in sources:
            held = arrays[chunks[0][0][0]].shape[0]
            inside = source[slot] - first
            first += held

            @pl.when((slot < count[0]) & (inside >= 0) & (inside < held))
            def _(chunks=chunks, inside=jnp.clip(inside, 0, held - 1)):
                left = 0
                for pieces in chunks:
                    rows = [arrays[number][inside, low:high, :] for number, low, high in pieces]
                    block = rows[0] if len(rows) == 1 else jnp.concatenate(rows, axis=0)
                    add(block, left)
                    left += block.shape[1]

    for output, (left, right, pieces) in zip(outputs, places):
        row = 0
        for start, stop, low, high in pieces:
            part = total[start:stop, low:high, left:right]
            output[:, row : row + high - low, :] = part.astype(BF16)
            row += high - low


def tile_sums(transposed, source, target, count, tiles, scale, arrays, sources, places, blocks):
    slots, size, _ = tiles.shape
    width = sum(arrays[pieces[0][0]].shape[2] for pieces in sources[0])
    smem = pl.BlockSpec(memory_space=pltpu.SMEM)
    vmem = pl.BlockSpec(memory_space=pltpu.VMEM)
    scaled = scale is not None
    operands = [tiles] + [scale] * scaled + list(arrays)
    shapes = [
        (pieces[0][1] - pieces[0][0], sum(high - low for _, _, low, high in pieces), right - left)
        for left, right, pieces in places
    ]
    return pl.pallas_call(
        functools.partial(tile_kernel, transposed, scaled, sources, places),
        out_shape=[jax.ShapeDtypeStruct(shape, BF16) for shape in shapes],
        in_specs=[smem] * 3 + [vmem] * len(operands),
        out_specs=[vmem] * len(shapes),
        scratch_shapes=[pltpu.VMEM((blocks, size, width), F32)],
        compiler_params=pltpu.CompilerParams(vmem_limit_bytes=40 * 1024 * 1024),
        cost_estimate=pl.CostEstimate(
            flops=2 * slots * size * size * width,
            bytes_accessed=6 * blocks * size * width,
            transcendentals=0,
        ),
    )(source, target, count, *operands)


def local(features, weight, cotangent, tile_rows, tile_cols, tile_count, tile_vals):
    span, width = features.shape
    n_z4, n_z1, n_core = lax.axis_size(Z4), lax.axis_size("z1"), lax.axis_size("core")
    n_y, n_zh, n_x = lax.axis_size("y"), lax.axis_size("zh"), lax.axis_size("x")
    n_line = n_z4 * n_z1
    n_row, n_col = n_line * n_core, n_y * n_zh * n_x
    n_plane = n_y * n_x
    my_row = lax.axis_index(ROW)
    my_zh = lax.axis_index("zh")
    slots = tile_vals.shape[2]
    nodes = n_row * n_col * span
    tiles = tile_vals[0, 0]
    count = tile_count[0]
    row_index = tile_rows[0, 0]
    col_index = tile_cols[0, 0]
    col_bits = col_index ^ my_row
    col_place = (col_bits & 1) * n_line + (col_bits & 2) * (n_z4 // 2)
    col_place = col_place + ((col_bits >> 2) & 1) * 2 + (col_bits >> 3)
    row_plane = (row_index >> 3) * n_x + (row_index & 3)
    row_place = (((row_index >> 2) & 1) ^ my_zh) * n_plane + row_plane

    alive = (jnp.arange(slots, dtype=jnp.int32) < count[0]).astype(F32)
    order_cols = (col_index[:, None] == jnp.arange(n_row, dtype=jnp.int32)[None, :]).astype(F32)
    col_sums = jnp.sum(tiles, axis=1, dtype=F32) * alive[:, None]
    degree_terms = jnp.einsum("sc,sj->cj", order_cols, col_sums, precision=lax.Precision.HIGHEST)
    high = lax.reduce_precision(degree_terms, 8, 7)
    pieces = jnp.stack([high, degree_terms - high]).astype(BF16)
    chunk = width // CHUNKS
    parts = [slice(c * chunk, (c + 1) * chunk) for c in range(CHUNKS)]
    held = [features[None, :, part] for part in parts]
    held[-1] = jnp.concatenate([held[-1], pieces.reshape(1, -1, chunk)], axis=1)
    for axis in Z4:
        held = [jnp.concatenate([part, flip(part, axis)]) for part in held]
    pairs = [flip(part, "z1") for part in held]
    groups = [held, pairs] + [[flip(part, "core") for part in group] for group in (held, pairs)]

    def degrees(part):
        return jnp.sum(part[:, span:].astype(F32).reshape(-1, n_row, span), axis=0)

    col_scale = lax.rsqrt(1.0 + sum(degrees(group[-1]) for group in groups))
    own_scale = lax.dynamic_index_in_dim(col_scale, my_row, axis=0, keepdims=False)
    slot_scale = col_scale[col_index]

    near_terms, far_terms = tile_sums(
        False,
        col_place,
        row_place,
        count,
        tiles,
        slot_scale,
        sum(groups, []),
        [[[(g * CHUNKS + c, 0, span)] for c in range(CHUNKS)] for g in range(len(groups))],
        [(0, width, [(0, n_plane, 0, span)]), (0, width, [(n_plane, n_col, 0, span)])],
        n_col,
    )
    far_sum = jnp.sum(swap_parts(far_terms, PLANE).astype(F32), axis=0).astype(BF16)
    near_group = swap_parts(after(near_terms, far_sum), PLANE)
    own_total = jnp.sum(near_group.astype(F32), axis=0) + flip(far_sum, "zh").astype(F32)

    output, normed, grad_pre, grad_own = layer_rows(own_total, cotangent, weight)

    lead = span // 4
    weight_terms = jnp.einsum("nf,ng->fg", normed, grad_pre, preferred_element_type=F32)
    weight_parts = weight_terms.astype(BF16).reshape(n_plane, width // n_plane, width)
    first_group = swap_parts(
        jnp.concatenate([copies_of(grad_own[:lead], PLANE), weight_parts], axis=1), PLANE
    )
    grad_rest = jnp.concatenate([grad_own[lead:], flip(grad_own, "zh")])
    last_group = swap_parts(copies_of(after(grad_rest, first_group), PLANE), PLANE)

    line_rows = jnp.sum(first_group[:, lead:].astype(F32), axis=0)
    for axis in ("zh", "core", "za", "zb", "z1"):
        line_rows = line_rows + flip(line_rows, axis)
    line_rows = line_rows * (1.0 / math.sqrt(nodes))
    last_group = after(last_group, line_rows)

    halves = tile_sums(
        True,
        row_place,
        col_place,
        count,
        tiles,
        None,
        [first_group, last_group],
        [[[(0, 0, lead), (1, 0, span - lead)]], [[(1, span - lead, 2 * span - lead)]]],
        [
            (part.start, part.stop, [(first, first + n_line, 0, span)])
            for first in (0, n_line)
            for part in parts
        ],
        n_row,
    )
    totals = [
        keep.astype(F32) + flip(send, "core").astype(F32)
        for keep, send in zip(halves[:CHUNKS], halves[CHUNKS:])
    ]
    along = jnp.concatenate([total[0, :8] for total in totals], axis=1)
    weight_rows = swap_parts(copies_of(jnp.concatenate([line_rows, along]), PLANE), PLANE)
    weight_grad = weight_rows[:, : line_rows.shape[0]].reshape(width, width)
    for axis in ("z1", "zb", "za"):
        totals = [total.astype(BF16) for total in totals]
        size = totals[0].shape[0] // 2
        totals = [
            total[:size].astype(F32) + flip(total[size:], axis).astype(F32) for total in totals
        ]
    feature_grad = jnp.concatenate([total[0] for total in totals], axis=1) * own_scale[:, None]
    return (output, weight_grad, feature_grad)


def solution(mesh):
    fine = Mesh(mesh.devices.reshape(2, 2, 2, 2, 4, 2, 4), AXES)
    nodes, row, col = P(AXES, None), ROW, ("y", "zh", "x")
    in_specs = (
        nodes,
        P(),
        nodes,
        P(row, col, None),
        P(row, col, None),
        P(row, col),
        P(row, col, None, None, None),
    )
    out_specs = (nodes, P(), nodes)
    return jax.shard_map(local, mesh=fine, in_specs=in_specs, out_specs=out_specs, check_vma=False)
```

```python
import functools
import math

import jax
import jax.numpy as jnp
from jax import lax
from jax.experimental import pallas as pl
from jax.experimental.pallas import tpu as pltpu
from jax.sharding import Mesh
from jax.sharding import PartitionSpec as P

AXES = ("za", "zb", "z1", "core", "y", "zh", "x")
Z4 = ("za", "zb")
ROW = ("za", "zb", "z1", "core")
PLANE = ("y", "x")
CHUNKS = 2
BF16 = jnp.bfloat16
F32 = jnp.float32


def layer_rows(row_total, grad_rows, weight):
    inv_rms = lax.rsqrt(jnp.mean(row_total * row_total, axis=1, keepdims=True) + 1e-06)
    norm_f32 = row_total * inv_rms
    normed = norm_f32.astype(BF16)
    pre_act = jnp.dot(normed, weight, preferred_element_type=F32)
    output = jax.nn.silu(pre_act).astype(BF16)
    sigmoid_pre = jax.nn.sigmoid(pre_act)
    act_slope = sigmoid_pre * (1.0 + pre_act * (1.0 - sigmoid_pre))
    grad_pre = (grad_rows.astype(F32) * act_slope).astype(BF16)
    grad_norm = jnp.einsum("ng,fg->nf", grad_pre, weight, preferred_element_type=F32)
    grad_z = (
        inv_rms * (grad_norm - norm_f32 * jnp.mean(grad_norm * norm_f32, axis=1, keepdims=True))
    ).astype(BF16)
    return (output, normed, grad_pre, grad_z)


def flip(block, axis):
    return lax.ppermute(block, axis, [(0, 1), (1, 0)])


def after(value, *others):
    return lax.optimization_barrier((value,) + others)[0]


def swap_parts(parts, axes):
    return lax.all_to_all(parts, axes, split_axis=0, concat_axis=0, tiled=True)


def copies_of(block, axes):
    return jnp.broadcast_to(block[None], (lax.axis_size(axes),) + block.shape)


def tile_kernel(transposed, scaled, sources, places, source, target, count, tiles, *refs):
    scale, refs = (refs[0], refs[1:]) if scaled else (None, refs)
    total = refs[-1]
    arrays, outputs = refs[: -1 - len(places)], refs[-1 - len(places) : -1]
    slots, size, _ = tiles.shape
    axis = 0 if transposed else 1
    total[...] = jnp.zeros_like(total)
    for slot in range(slots):

        def add(block, left):
            if scaled:
                row = jnp.broadcast_to(scale[slot : slot + 1, :], (size, size))
                column = jnp.transpose(row)
                lanes = [block[:, i : i + size] for i in range(0, block.shape[1], size)]
                lanes = [(part.astype(F32) * column).astype(BF16) for part in lanes]
                block = jnp.concatenate(lanes, axis=1)
            total[target[slot], :, left : left + block.shape[1]] += lax.dot_general(
                tiles[slot], block, (((axis,), (0,)), ((), ())), preferred_element_type=F32
            )

        first = 0
        for chunks in sources:
            held = arrays[chunks[0][0][0]].shape[0]
            inside = source[slot] - first
            first += held

            @pl.when((slot < count[0]) & (inside >= 0) & (inside < held))
            def _(chunks=chunks, inside=jnp.clip(inside, 0, held - 1)):
                left = 0
                for pieces in chunks:
                    rows = [arrays[number][inside, low:high, :] for number, low, high in pieces]
                    block = rows[0] if len(rows) == 1 else jnp.concatenate(rows, axis=0)
                    add(block, left)
                    left += block.shape[1]

    for output, (left, right, pieces) in zip(outputs, places):
        row = 0
        for start, stop, low, high in pieces:
            part = total[start:stop, low:high, left:right]
            output[:, row : row + high - low, :] = part.astype(BF16)
            row += high - low


def tile_sums(transposed, source, target, count, tiles, scale, arrays, sources, places, blocks):
    slots, size, _ = tiles.shape
    width = sum(arrays[pieces[0][0]].shape[2] for pieces in sources[0])
    smem = pl.BlockSpec(memory_space=pltpu.SMEM)
    vmem = pl.BlockSpec(memory_space=pltpu.VMEM)
    scaled = scale is not None
    operands = [tiles] + [scale] * scaled + list(arrays)
    shapes = [
        (pieces[0][1] - pieces[0][0], sum(high - low for _, _, low, high in pieces), right - left)
        for left, right, pieces in places
    ]
    return pl.pallas_call(
        functools.partial(tile_kernel, transposed, scaled, sources, places),
        out_shape=[jax.ShapeDtypeStruct(shape, BF16) for shape in shapes],
        in_specs=[smem] * 3 + [vmem] * len(operands),
        out_specs=[vmem] * len(shapes),
        scratch_shapes=[pltpu.VMEM((blocks, size, width), F32)],
        compiler_params=pltpu.CompilerParams(vmem_limit_bytes=40 * 1024 * 1024),
        cost_estimate=pl.CostEstimate(
            flops=2 * slots * size * size * width,
            bytes_accessed=6 * blocks * size * width,
            transcendentals=0,
        ),
    )(source, target, count, *operands)


def local(features, weight, cotangent, tile_rows, tile_cols, tile_count, tile_vals):
    span, width = features.shape
    n_z4, n_z1, n_core = lax.axis_size(Z4), lax.axis_size("z1"), lax.axis_size("core")
    n_y, n_zh, n_x = lax.axis_size("y"), lax.axis_size("zh"), lax.axis_size("x")
    n_line = n_z4 * n_z1
    n_row, n_col = n_line * n_core, n_y * n_zh * n_x
    n_plane = n_y * n_x
    my_row = lax.axis_index(ROW)
    my_zh = lax.axis_index("zh")
    slots = tile_vals.shape[2]
    nodes = n_row * n_col * span
    tiles = tile_vals[0, 0]
    count = tile_count[0]
    row_index = tile_rows[0, 0]
    col_index = tile_cols[0, 0]
    col_bits = col_index ^ my_row
    col_place = (col_bits & 1) * n_line + (col_bits & 2) * (n_z4 // 2)
    col_from = col_place + ((col_bits >> 2) & 1) * 2 + (col_bits >> 3)
    col_to = col_place + (col_index >> 2)
    row_plane = (row_index >> 3) * n_x + (row_index & 3)
    row_place = (((row_index >> 2) & 1) ^ my_zh) * n_plane + row_plane

    alive = (jnp.arange(slots, dtype=jnp.int32) < count[0]).astype(F32)
    order_cols = (col_index[:, None] == jnp.arange(n_row, dtype=jnp.int32)[None, :]).astype(F32)
    col_sums = jnp.sum(tiles, axis=1, dtype=F32) * alive[:, None]
    degree_terms = jnp.einsum("sc,sj->cj", order_cols, col_sums, precision=lax.Precision.HIGHEST)
    high = lax.reduce_precision(degree_terms, 8, 7)
    pieces = jnp.stack([high, degree_terms - high]).astype(BF16)
    chunk = width // CHUNKS
    parts = [slice(c * chunk, (c + 1) * chunk) for c in range(CHUNKS)]
    held = [features[None, :, part] for part in parts]
    held[-1] = jnp.concatenate([held[-1], pieces.reshape(1, -1, chunk)], axis=1)
    for axis in Z4:
        held = [jnp.concatenate([part, flip(part, axis)]) for part in held]
    pairs = [flip(part, "z1") for part in held]
    groups = [held, pairs] + [[flip(part, "core") for part in group] for group in (held, pairs)]

    def degrees(part):
        return jnp.sum(part[:, span:].astype(F32).reshape(-1, n_row, span), axis=0)

    col_scale = lax.rsqrt(1.0 + sum(degrees(group[-1]) for group in groups))
    own_scale = lax.dynamic_index_in_dim(col_scale, my_row, axis=0, keepdims=False)
    slot_scale = col_scale[col_index]

    near_terms, far_terms = tile_sums(
        False,
        col_from,
        row_place,
        count,
        tiles,
        slot_scale,
        sum(groups, []),
        [[[(g * CHUNKS + c, 0, span)] for c in range(CHUNKS)] for g in range(len(groups))],
        [(0, width, [(0, n_plane, 0, span)]), (0, width, [(n_plane, n_col, 0, span)])],
        n_col,
    )
    far_sum = jnp.sum(swap_parts(far_terms, PLANE).astype(F32), axis=0).astype(BF16)
    near_group = swap_parts(after(near_terms, far_sum), PLANE)
    own_total = jnp.sum(near_group.astype(F32), axis=0) + flip(far_sum, "zh").astype(F32)

    output, normed, grad_pre, grad_own = layer_rows(own_total, cotangent, weight)

    lead = span // 4
    weight_terms = jnp.einsum("nf,ng->fg", normed, grad_pre, preferred_element_type=F32)
    weight_parts = weight_terms.astype(BF16).reshape(n_plane, width // n_plane, width)
    first_group = swap_parts(
        jnp.concatenate([copies_of(grad_own[:lead], PLANE), weight_parts], axis=1), PLANE
    )
    grad_rest = jnp.concatenate([grad_own[lead:], flip(grad_own, "zh")])
    last_group = swap_parts(copies_of(after(grad_rest, first_group), PLANE), PLANE)

    line_rows = jnp.sum(first_group[:, lead:].astype(F32), axis=0)
    for axis in ("zh", "core", "za", "zb", "z1"):
        line_rows = line_rows + flip(line_rows, axis)
    line_rows = line_rows * (1.0 / math.sqrt(nodes))
    last_group = after(last_group, line_rows)

    halves = tile_sums(
        True,
        row_place,
        col_to,
        count,
        tiles,
        None,
        [first_group, last_group],
        [[[(0, 0, lead), (1, 0, span - lead)]], [[(1, span - lead, 2 * span - lead)]]],
        [
            (part.start, part.stop, [(first, first + n_line, 0, span)])
            for first in (0, n_line)
            for part in parts
        ],
        n_row,
    )
    totals = [
        keep.astype(F32) + flip(send, "core").astype(F32)
        for keep, send in zip(halves[:CHUNKS], halves[CHUNKS:])
    ]
    weight_grad = swap_parts(copies_of(line_rows, PLANE), PLANE).reshape(width, width)
    totals = [total.astype(BF16) for total in totals]
    totals = [
        total[:n_z4].astype(F32) + flip(total[n_z4:], "z1").astype(F32) for total in totals
    ]
    pair_sum = jnp.concatenate([total.astype(BF16) for total in totals], axis=2)
    own_grad = jnp.sum(swap_parts(pair_sum, Z4).astype(F32), axis=0)
    feature_grad = own_grad * own_scale[:, None]
    return (output, weight_grad, feature_grad)


def solution(mesh):
    fine = Mesh(mesh.devices.reshape(2, 2, 2, 2, 4, 2, 4), AXES)
    nodes, row, col = P(AXES, None), ROW, ("y", "zh", "x")
    in_specs = (
        nodes,
        P(),
        nodes,
        P(row, col, None),
        P(row, col, None),
        P(row, col),
        P(row, col, None, None, None),
    )
    out_specs = (nodes, P(), nodes)
    return jax.shard_map(local, mesh=fine, in_specs=in_specs, out_specs=out_specs, check_vma=False)
```

```python
import functools
import math

import jax
import jax.numpy as jnp
from jax import lax
from jax.experimental import pallas as pl
from jax.experimental.pallas import tpu as pltpu
from jax.sharding import Mesh
from jax.sharding import PartitionSpec as P

AXES = ("za", "zb", "z1", "core", "y", "zh", "x")
Z4 = ("za", "zb")
ROW = ("za", "zb", "z1", "core")
PLANE = ("y", "x")
CHUNKS = 2
BF16 = jnp.bfloat16
F32 = jnp.float32


def layer_rows(row_total, grad_rows, weight):
    inv_rms = lax.rsqrt(jnp.mean(row_total * row_total, axis=1, keepdims=True) + 1e-06)
    norm_f32 = row_total * inv_rms
    normed = norm_f32.astype(BF16)
    pre_act = jnp.dot(normed, weight, preferred_element_type=F32)
    output = jax.nn.silu(pre_act).astype(BF16)
    sigmoid_pre = jax.nn.sigmoid(pre_act)
    act_slope = sigmoid_pre * (1.0 + pre_act * (1.0 - sigmoid_pre))
    grad_pre = (grad_rows.astype(F32) * act_slope).astype(BF16)
    grad_norm = jnp.einsum("ng,fg->nf", grad_pre, weight, preferred_element_type=F32)
    grad_z = (
        inv_rms * (grad_norm - norm_f32 * jnp.mean(grad_norm * norm_f32, axis=1, keepdims=True))
    ).astype(BF16)
    return (output, normed, grad_pre, grad_z)


def flip(block, axis):
    return lax.ppermute(block, axis, [(0, 1), (1, 0)])


def after(value, *others):
    return lax.optimization_barrier((value,) + others)[0]


def swap_parts(parts, axes):
    return lax.all_to_all(parts, axes, split_axis=0, concat_axis=0, tiled=True)


def copies_of(block, axes):
    return jnp.broadcast_to(block[None], (lax.axis_size(axes),) + block.shape)


def tile_kernel(transposed, scaled, sources, places, source, target, count, tiles, *refs):
    scale, refs = (refs[0], refs[1:]) if scaled else (None, refs)
    total = refs[-1]
    arrays, outputs = refs[: -1 - len(places)], refs[-1 - len(places) : -1]
    slots, size, _ = tiles.shape
    axis = 0 if transposed else 1
    for output in outputs:
        output[...] = jnp.zeros_like(output)
    total[...] = jnp.zeros_like(total)
    owners = []
    for slot in range(slots):
        owner = jnp.int32(slot)
        for earlier in reversed(range(slot)):
            owner = jnp.where(target[earlier] == target[slot], earlier, owner)
        owners.append(owner)

    for slot in range(slots):

        def add(block, left):
            if scaled:
                row = jnp.broadcast_to(scale[slot : slot + 1, :], (size, size))
                column = jnp.transpose(row)
                lanes = [block[:, i : i + size] for i in range(0, block.shape[1], size)]
                lanes = [(part.astype(F32) * column).astype(BF16) for part in lanes]
                block = jnp.concatenate(lanes, axis=1)
            total[owners[slot], :, left : left + block.shape[1]] += lax.dot_general(
                tiles[slot], block, (((axis,), (0,)), ((), ())), preferred_element_type=F32
            )

        first = 0
        for chunks in sources:
            held = arrays[chunks[0][0][0]].shape[0]
            inside = source[slot] - first
            first += held

            @pl.when((slot < count[0]) & (inside >= 0) & (inside < held))
            def _(chunks=chunks, inside=jnp.clip(inside, 0, held - 1)):
                left = 0
                for pieces in chunks:
                    rows = [arrays[number][inside, low:high, :] for number, low, high in pieces]
                    block = rows[0] if len(rows) == 1 else jnp.concatenate(rows, axis=0)
                    add(block, left)
                    left += block.shape[1]

    for slot in range(slots):
        for output, (left, right, start, stop) in zip(outputs, places):
            place = target[slot] - start
            held = (place >= 0) & (place < stop - start)

            @pl.when((slot < count[0]) & (owners[slot] == slot) & held)
            def _(output=output, left=left, right=right, place=jnp.clip(place, 0, stop - start - 1)):
                output[place] = total[slot, :, left:right].astype(BF16)


def tile_sums(transposed, source, target, count, tiles, scale, arrays, sources, places):
    slots, size, _ = tiles.shape
    width = sum(arrays[pieces[0][0]].shape[2] for pieces in sources[0])
    smem = pl.BlockSpec(memory_space=pltpu.SMEM)
    vmem = pl.BlockSpec(memory_space=pltpu.VMEM)
    scaled = scale is not None
    operands = [tiles] + [scale] * scaled + list(arrays)
    shapes = [(stop - start, size, right - left) for left, right, start, stop in places]
    moved = sum(math.prod(shape) for shape in shapes) + sum(array.size for array in arrays)
    return pl.pallas_call(
        functools.partial(tile_kernel, transposed, scaled, sources, places),
        out_shape=[jax.ShapeDtypeStruct(shape, BF16) for shape in shapes],
        in_specs=[smem] * 3 + [vmem] * len(operands),
        out_specs=[vmem] * len(shapes),
        scratch_shapes=[pltpu.VMEM((slots, size, width), F32)],
        compiler_params=pltpu.CompilerParams(vmem_limit_bytes=40 * 1024 * 1024),
        cost_estimate=pl.CostEstimate(
            flops=2 * slots * size * size * width,
            bytes_accessed=2 * moved,
            transcendentals=0,
        ),
    )(source, target, count, *operands)


def local(features, weight, cotangent, tile_rows, tile_cols, tile_count, tile_vals):
    span, width = features.shape
    n_z4, n_z1, n_core = lax.axis_size(Z4), lax.axis_size("z1"), lax.axis_size("core")
    n_y, n_zh, n_x = lax.axis_size("y"), lax.axis_size("zh"), lax.axis_size("x")
    n_line = n_z4 * n_z1
    n_row, n_col = n_line * n_core, n_y * n_zh * n_x
    n_plane = n_y * n_x
    my_row = lax.axis_index(ROW)
    my_zh = lax.axis_index("zh")
    slots = tile_vals.shape[2]
    nodes = n_row * n_col * span
    tiles = tile_vals[0, 0]
    count = tile_count[0]
    row_index = tile_rows[0, 0]
    col_index = tile_cols[0, 0]
    col_bits = col_index ^ my_row
    col_place = (col_bits & 1) * n_line + (col_bits & 2) * (n_z4 // 2)
    col_place = col_place + ((col_bits >> 2) & 1) * 2 + (col_bits >> 3)
    row_plane = (row_index >> 3) * n_x + (row_index & 3)
    row_place = (((row_index >> 2) & 1) ^ my_zh) * n_plane + row_plane

    alive = (jnp.arange(slots, dtype=jnp.int32) < count[0]).astype(F32)
    order_cols = (col_index[:, None] == jnp.arange(n_row, dtype=jnp.int32)[None, :]).astype(F32)
    col_sums = jnp.sum(tiles, axis=1, dtype=F32) * alive[:, None]
    degree_terms = jnp.einsum("sc,sj->cj", order_cols, col_sums, precision=lax.Precision.HIGHEST)
    high = lax.reduce_precision(degree_terms, 8, 7)
    pieces = jnp.stack([high, degree_terms - high]).astype(BF16)
    chunk = width // CHUNKS
    parts = [slice(c * chunk, (c + 1) * chunk) for c in range(CHUNKS)]
    held = [features[None, :, part] for part in parts]
    held[0] = jnp.concatenate([held[0], pieces.reshape(1, -1, chunk)], axis=1)
    for axis in Z4:
        held = [jnp.concatenate([part, flip(part, axis)]) for part in held]
    pairs = [flip(part, "z1") for part in held]
    groups = [held, pairs] + [[flip(part, "core") for part in group] for group in (held, pairs)]

    def degrees(part):
        return jnp.sum(part[:, span:].astype(F32).reshape(-1, n_row, span), axis=0)

    col_scale = lax.rsqrt(1.0 + sum(degrees(group[0]) for group in groups))
    own_scale = lax.dynamic_index_in_dim(col_scale, my_row, axis=0, keepdims=False)
    slot_scale = col_scale[col_index]

    near_terms, far_terms = tile_sums(
        False,
        col_place,
        row_place,
        count,
        tiles,
        slot_scale,
        sum(groups, []),
        [[[(g * CHUNKS + c, 0, span)] for c in range(CHUNKS)] for g in range(len(groups))],
        [(0, width, 0, n_plane), (0, width, n_plane, n_col)],
    )
    far_sum = jnp.sum(swap_parts(far_terms, PLANE).astype(F32), axis=0).astype(BF16)
    near_group = swap_parts(after(near_terms, far_sum), PLANE)
    own_total = jnp.sum(near_group.astype(F32), axis=0) + flip(far_sum, "zh").astype(F32)

    output, normed, grad_pre, grad_own = layer_rows(own_total, cotangent, weight)

    lead = span // 4
    weight_terms = jnp.einsum("nf,ng->fg", normed, grad_pre, preferred_element_type=F32)
    weight_parts = weight_terms.astype(BF16).reshape(n_plane, width // n_plane, width)
    first_group = swap_parts(
        jnp.concatenate([copies_of(grad_own[:lead], PLANE), weight_parts], axis=1), PLANE
    )
    grad_rest = jnp.concatenate([grad_own[lead:], flip(grad_own, "zh")])
    last_group = swap_parts(copies_of(after(grad_rest, first_group), PLANE), PLANE)

    line_rows = jnp.sum(first_group[:, lead:].astype(F32), axis=0)
    for axis in ("core", "z1", "zb", "za", "zh"):
        line_rows = line_rows + flip(line_rows, axis)
    line_rows = line_rows * (1.0 / math.sqrt(nodes))
    last_group = after(last_group, line_rows)

    halves = tile_sums(
        True,
        row_place,
        col_place,
        count,
        tiles,
        None,
        [first_group, last_group],
        [[[(0, 0, lead), (1, 0, span - lead)]], [[(1, span - lead, 2 * span - lead)]]],
        [(part.start, part.stop, first, first + n_line) for first in (0, n_line) for part in parts],
    )
    totals = [
        keep.astype(F32) + flip(send, "core").astype(F32)
        for keep, send in zip(halves[:CHUNKS], halves[CHUNKS:])
    ]
    along = jnp.concatenate([total[0, :8] for total in totals], axis=1)
    weight_rows = swap_parts(copies_of(jnp.concatenate([line_rows, along]), PLANE), PLANE)
    weight_grad = weight_rows[:, : line_rows.shape[0]].reshape(width, width)
    for axis in ("z1", "zb", "za"):
        totals = [total.astype(BF16) for total in totals]
        size = totals[0].shape[0] // 2
        totals = [
            total[:size].astype(F32) + flip(total[size:], axis).astype(F32) for total in totals
        ]
    feature_grad = jnp.concatenate([total[0] for total in totals], axis=1) * own_scale[:, None]
    return (output, weight_grad, feature_grad)


def solution(mesh):
    fine = Mesh(mesh.devices.reshape(2, 2, 2, 2, 4, 2, 4), AXES)
    nodes, row, col = P(AXES, None), ROW, ("y", "zh", "x")
    in_specs = (
        nodes,
        P(),
        nodes,
        P(row, col, None),
        P(row, col, None),
        P(row, col),
        P(row, col, None, None, None),
    )
    out_specs = (nodes, P(), nodes)
    return jax.shard_map(local, mesh=fine, in_specs=in_specs, out_specs=out_specs, check_vma=False)
```

```python
import functools
import math

import jax
import jax.numpy as jnp
from jax import lax
from jax.experimental import pallas as pl
from jax.experimental.pallas import tpu as pltpu
from jax.sharding import Mesh
from jax.sharding import PartitionSpec as P

AXES = ("za", "zb", "z1", "core", "y", "zh", "x")
Z4 = ("za", "zb")
ROW = ("za", "zb", "z1", "core")
PLANE = ("y", "x")
CHUNKS = 2
BF16 = jnp.bfloat16
F32 = jnp.float32


def layer_rows(row_total, grad_rows, weight):
    inv_rms = lax.rsqrt(jnp.mean(row_total * row_total, axis=1, keepdims=True) + 1e-06)
    norm_f32 = row_total * inv_rms
    normed = norm_f32.astype(BF16)
    pre_act = jnp.dot(normed, weight, preferred_element_type=F32)
    output = jax.nn.silu(pre_act).astype(BF16)
    sigmoid_pre = jax.nn.sigmoid(pre_act)
    act_slope = sigmoid_pre * (1.0 + pre_act * (1.0 - sigmoid_pre))
    grad_pre = (grad_rows.astype(F32) * act_slope).astype(BF16)
    grad_norm = jnp.einsum("ng,fg->nf", grad_pre, weight, preferred_element_type=F32)
    grad_z = (
        inv_rms * (grad_norm - norm_f32 * jnp.mean(grad_norm * norm_f32, axis=1, keepdims=True))
    ).astype(BF16)
    return (output, normed, grad_pre, grad_z)


def flip(block, axis):
    return lax.ppermute(block, axis, [(0, 1), (1, 0)])


def after(value, *others):
    return lax.optimization_barrier((value,) + others)[0]


def swap_parts(parts, axes):
    return lax.all_to_all(parts, axes, split_axis=0, concat_axis=0, tiled=True)


def copies_of(block, axes):
    return jnp.broadcast_to(block[None], (lax.axis_size(axes),) + block.shape)


def tile_kernel(transposed, scaled, sources, places, source, target, count, tiles, *refs):
    scale, refs = (refs[0], refs[1:]) if scaled else (None, refs)
    total = refs[-1]
    arrays, outputs = refs[: -1 - len(places)], refs[-1 - len(places) : -1]
    slots, size, _ = tiles.shape
    axis = 0 if transposed else 1
    for output in outputs:
        output[...] = jnp.zeros_like(output)
    total[...] = jnp.zeros_like(total)
    owners = []
    for slot in range(slots):
        owner = jnp.int32(slot)
        for earlier in reversed(range(slot)):
            owner = jnp.where(target[earlier] == target[slot], earlier, owner)
        owners.append(owner)

    for slot in range(slots):

        def add(block, left):
            if scaled:
                row = jnp.broadcast_to(scale[slot : slot + 1, :], (size, size))
                column = jnp.transpose(row)
                lanes = [block[:, i : i + size] for i in range(0, block.shape[1], size)]
                lanes = [(part.astype(F32) * column).astype(BF16) for part in lanes]
                block = jnp.concatenate(lanes, axis=1)
            total[owners[slot], :, left : left + block.shape[1]] += lax.dot_general(
                tiles[slot], block, (((axis,), (0,)), ((), ())), preferred_element_type=F32
            )

        first = 0
        for chunks in sources:
            held = arrays[chunks[0][0][0]].shape[0]
            inside = source[slot] - first
            first += held

            @pl.when((slot < count[0]) & (inside >= 0) & (inside < held))
            def _(chunks=chunks, inside=jnp.clip(inside, 0, held - 1)):
                left = 0
                for pieces in chunks:
                    rows = [arrays[number][inside, low:high, :] for number, low, high in pieces]
                    block = rows[0] if len(rows) == 1 else jnp.concatenate(rows, axis=0)
                    add(block, left)
                    left += block.shape[1]

    for slot in range(slots):
        for output, (left, right, start, stop) in zip(outputs, places):
            place = target[slot] - start
            held = (place >= 0) & (place < stop - start)

            @pl.when((slot < count[0]) & (owners[slot] == slot) & held)
            def _(output=output, left=left, right=right, place=jnp.clip(place, 0, stop - start - 1)):
                output[place] = total[slot, :, left:right].astype(BF16)


def tile_sums(transposed, source, target, count, tiles, scale, arrays, sources, places):
    slots, size, _ = tiles.shape
    width = sum(arrays[pieces[0][0]].shape[2] for pieces in sources[0])
    smem = pl.BlockSpec(memory_space=pltpu.SMEM)
    vmem = pl.BlockSpec(memory_space=pltpu.VMEM)
    scaled = scale is not None
    operands = [tiles] + [scale] * scaled + list(arrays)
    shapes = [(stop - start, size, right - left) for left, right, start, stop in places]
    moved = sum(math.prod(shape) for shape in shapes) + sum(array.size for array in arrays)
    return pl.pallas_call(
        functools.partial(tile_kernel, transposed, scaled, sources, places),
        out_shape=[jax.ShapeDtypeStruct(shape, BF16) for shape in shapes],
        in_specs=[smem] * 3 + [vmem] * len(operands),
        out_specs=[vmem] * len(shapes),
        scratch_shapes=[pltpu.VMEM((slots, size, width), F32)],
        compiler_params=pltpu.CompilerParams(vmem_limit_bytes=40 * 1024 * 1024),
        cost_estimate=pl.CostEstimate(
            flops=2 * slots * size * size * width,
            bytes_accessed=2 * moved,
            transcendentals=0,
        ),
    )(source, target, count, *operands)


def local(features, weight, cotangent, tile_rows, tile_cols, tile_count, tile_vals):
    span, width = features.shape
    n_z4, n_z1, n_core = lax.axis_size(Z4), lax.axis_size("z1"), lax.axis_size("core")
    n_y, n_zh, n_x = lax.axis_size("y"), lax.axis_size("zh"), lax.axis_size("x")
    n_line = n_z4 * n_z1
    n_row, n_col = n_line * n_core, n_y * n_zh * n_x
    n_plane = n_y * n_x
    my_row = lax.axis_index(ROW)
    my_zh = lax.axis_index("zh")
    slots = tile_vals.shape[2]
    nodes = n_row * n_col * span
    tiles = tile_vals[0, 0]
    count = tile_count[0]
    row_index = tile_rows[0, 0]
    col_index = tile_cols[0, 0]
    col_bits = col_index ^ my_row
    col_place = (col_bits & 1) * n_line + (col_bits & 2) * (n_z4 // 2)
    col_place = col_place + ((col_bits >> 2) & 1) * 2 + (col_bits >> 3)
    row_plane = (row_index >> 3) * n_x + (row_index & 3)
    row_place = (((row_index >> 2) & 1) ^ my_zh) * n_plane + row_plane

    alive = (jnp.arange(slots, dtype=jnp.int32) < count[0]).astype(F32)
    order_cols = (col_index[:, None] == jnp.arange(n_row, dtype=jnp.int32)[None, :]).astype(F32)
    col_sums = jnp.sum(tiles, axis=1, dtype=F32) * alive[:, None]
    degree_terms = jnp.einsum("sc,sj->cj", order_cols, col_sums, precision=lax.Precision.HIGHEST)
    high = lax.reduce_precision(degree_terms, 8, 7)
    pieces = jnp.stack([high, degree_terms - high]).astype(BF16)
    chunk = width // CHUNKS
    parts = [slice(c * chunk, (c + 1) * chunk) for c in range(CHUNKS)]
    held = [features[None, :, part] for part in parts]
    held[0] = jnp.concatenate([held[0], pieces.reshape(1, -1, chunk)], axis=1)
    for axis in Z4:
        held = [jnp.concatenate([part, flip(part, axis)]) for part in held]
    pairs = [flip(part, "z1") for part in held]
    groups = [held, pairs] + [[flip(part, "core") for part in group] for group in (held, pairs)]

    def degrees(part):
        return jnp.sum(part[:, span:].astype(F32).reshape(-1, n_row, span), axis=0)

    col_scale = lax.rsqrt(1.0 + sum(degrees(group[0]) for group in groups))
    own_scale = lax.dynamic_index_in_dim(col_scale, my_row, axis=0, keepdims=False)
    slot_scale = col_scale[col_index]

    near_terms, far_terms = tile_sums(
        False,
        col_place,
        row_place,
        count,
        tiles,
        slot_scale,
        sum(groups, []),
        [[[(g * CHUNKS + c, 0, span)] for c in range(CHUNKS)] for g in range(len(groups))],
        [(0, width, 0, n_plane), (0, width, n_plane, n_col)],
    )
    far_sum = jnp.sum(swap_parts(far_terms, PLANE).astype(F32), axis=0).astype(BF16)
    near_group = swap_parts(after(near_terms, far_sum), PLANE)
    own_total = jnp.sum(near_group.astype(F32), axis=0) + flip(far_sum, "zh").astype(F32)

    output, normed, grad_pre, grad_own = layer_rows(own_total, cotangent, weight)

    lead = span * 3 // 8
    weight_terms = jnp.einsum("nf,ng->fg", normed, grad_pre, preferred_element_type=F32)
    weight_parts = weight_terms.astype(BF16).reshape(n_plane, width // n_plane, width)
    first_group = swap_parts(
        jnp.concatenate([copies_of(grad_own[:lead], PLANE), weight_parts], axis=1), PLANE
    )
    grad_rest = jnp.concatenate([grad_own[lead:], flip(grad_own, "zh")])
    last_group = swap_parts(copies_of(after(grad_rest, first_group), PLANE), PLANE)

    line_rows = jnp.sum(first_group[:, lead:].astype(F32), axis=0)
    for axis in ("core", "z1", "zb", "za", "zh"):
        line_rows = line_rows + flip(line_rows, axis)
    line_rows = line_rows * (1.0 / math.sqrt(nodes))
    last_group = after(last_group, line_rows)

    halves = tile_sums(
        True,
        row_place,
        col_place,
        count,
        tiles,
        None,
        [first_group, last_group],
        [[[(0, 0, lead), (1, 0, span - lead)]], [[(1, span - lead, 2 * span - lead)]]],
        [(part.start, part.stop, first, first + n_line) for first in (0, n_line) for part in parts],
    )
    totals = [
        keep.astype(F32) + flip(send, "core").astype(F32)
        for keep, send in zip(halves[:CHUNKS], halves[CHUNKS:])
    ]
    along = jnp.concatenate([total[0, :8] for total in totals], axis=1)
    weight_rows = swap_parts(copies_of(jnp.concatenate([line_rows, along]), PLANE), PLANE)
    weight_grad = weight_rows[:, : line_rows.shape[0]].reshape(width, width)
    for axis in ("z1", "zb", "za"):
        totals = [total.astype(BF16) for total in totals]
        size = totals[0].shape[0] // 2
        totals = [
            total[:size].astype(F32) + flip(total[size:], axis).astype(F32) for total in totals
        ]
    feature_grad = jnp.concatenate([total[0] for total in totals], axis=1) * own_scale[:, None]
    return (output, weight_grad, feature_grad)


def solution(mesh):
    fine = Mesh(mesh.devices.reshape(2, 2, 2, 2, 4, 2, 4), AXES)
    nodes, row, col = P(AXES, None), ROW, ("y", "zh", "x")
    in_specs = (
        nodes,
        P(),
        nodes,
        P(row, col, None),
        P(row, col, None),
        P(row, col),
        P(row, col, None, None, None),
    )
    out_specs = (nodes, P(), nodes)
    return jax.shard_map(local, mesh=fine, in_specs=in_specs, out_specs=out_specs, check_vma=False)
```

```python
import functools
import math

import jax
import jax.numpy as jnp
from jax import lax
from jax.experimental import pallas as pl
from jax.experimental.pallas import tpu as pltpu
from jax.sharding import Mesh
from jax.sharding import PartitionSpec as P

AXES = ("za", "zb", "z1", "core", "y", "zh", "x")
Z4 = ("za", "zb")
ROW = ("za", "zb", "z1", "core")
PLANE = ("y", "x")
CHUNKS = 2
BF16 = jnp.bfloat16
F32 = jnp.float32


def layer_rows(row_total, grad_rows, weight):
    inv_rms = lax.rsqrt(jnp.mean(row_total * row_total, axis=1, keepdims=True) + 1e-06)
    norm_f32 = row_total * inv_rms
    normed = norm_f32.astype(BF16)
    pre_act = jnp.dot(normed, weight, preferred_element_type=F32)
    output = jax.nn.silu(pre_act).astype(BF16)
    sigmoid_pre = jax.nn.sigmoid(pre_act)
    act_slope = sigmoid_pre * (1.0 + pre_act * (1.0 - sigmoid_pre))
    grad_pre = (grad_rows.astype(F32) * act_slope).astype(BF16)
    grad_norm = jnp.einsum("ng,fg->nf", grad_pre, weight, preferred_element_type=F32)
    grad_z = (
        inv_rms * (grad_norm - norm_f32 * jnp.mean(grad_norm * norm_f32, axis=1, keepdims=True))
    ).astype(BF16)
    return (output, normed, grad_pre, grad_z)


def flip(block, axis):
    return lax.ppermute(block, axis, [(0, 1), (1, 0)])


def after(value, *others):
    return lax.optimization_barrier((value,) + others)[0]


def swap_parts(parts, axes):
    return lax.all_to_all(parts, axes, split_axis=0, concat_axis=0, tiled=True)


def copies_of(block, axes):
    return jnp.broadcast_to(block[None], (lax.axis_size(axes),) + block.shape)


def tile_kernel(transposed, scaled, sources, places, source, target, count, tiles, *refs):
    scale, refs = (refs[0], refs[1:]) if scaled else (None, refs)
    total = refs[-1]
    arrays, outputs = refs[: -1 - len(places)], refs[-1 - len(places) : -1]
    slots, size, _ = tiles.shape
    axis = 0 if transposed else 1
    for output in outputs:
        output[...] = jnp.zeros_like(output)
    total[...] = jnp.zeros_like(total)
    owners = []
    for slot in range(slots):
        owner = jnp.int32(slot)
        for earlier in reversed(range(slot)):
            owner = jnp.where(target[earlier] == target[slot], earlier, owner)
        owners.append(owner)

    for slot in range(slots):

        def add(block, left):
            if scaled:
                row = jnp.broadcast_to(scale[slot : slot + 1, :], (size, size))
                column = jnp.transpose(row)
                lanes = [block[:, i : i + size] for i in range(0, block.shape[1], size)]
                lanes = [(part.astype(F32) * column).astype(BF16) for part in lanes]
                block = jnp.concatenate(lanes, axis=1)
            total[owners[slot], :, left : left + block.shape[1]] += lax.dot_general(
                tiles[slot], block, (((axis,), (0,)), ((), ())), preferred_element_type=F32
            )

        first = 0
        for chunks in sources:
            held = arrays[chunks[0][0][0]].shape[0]
            inside = source[slot] - first
            first += held

            @pl.when((slot < count[0]) & (inside >= 0) & (inside < held))
            def _(chunks=chunks, inside=jnp.clip(inside, 0, held - 1)):
                left = 0
                for pieces in chunks:
                    rows = [arrays[number][inside, low:high, :] for number, low, high in pieces]
                    block = rows[0] if len(rows) == 1 else jnp.concatenate(rows, axis=0)
                    add(block, left)
                    left += block.shape[1]

    for slot in range(slots):
        for output, (left, right, start, stop) in zip(outputs, places):
            place = target[slot] - start
            held = (place >= 0) & (place < stop - start)

            @pl.when((slot < count[0]) & (owners[slot] == slot) & held)
            def _(output=output, left=left, right=right, place=jnp.clip(place, 0, stop - start - 1)):
                output[place] = total[slot, :, left:right].astype(BF16)


def tile_sums(transposed, source, target, count, tiles, scale, arrays, sources, places):
    slots, size, _ = tiles.shape
    width = sum(arrays[pieces[0][0]].shape[2] for pieces in sources[0])
    smem = pl.BlockSpec(memory_space=pltpu.SMEM)
    vmem = pl.BlockSpec(memory_space=pltpu.VMEM)
    scaled = scale is not None
    operands = [tiles] + [scale] * scaled + list(arrays)
    shapes = [(stop - start, size, right - left) for left, right, start, stop in places]
    moved = sum(math.prod(shape) for shape in shapes) + sum(array.size for array in arrays)
    return pl.pallas_call(
        functools.partial(tile_kernel, transposed, scaled, sources, places),
        out_shape=[jax.ShapeDtypeStruct(shape, BF16) for shape in shapes],
        in_specs=[smem] * 3 + [vmem] * len(operands),
        out_specs=[vmem] * len(shapes),
        scratch_shapes=[pltpu.VMEM((slots, size, width), F32)],
        compiler_params=pltpu.CompilerParams(vmem_limit_bytes=40 * 1024 * 1024),
        cost_estimate=pl.CostEstimate(
            flops=2 * slots * size * size * width,
            bytes_accessed=2 * moved,
            transcendentals=0,
        ),
    )(source, target, count, *operands)


def local(features, weight, cotangent, tile_rows, tile_cols, tile_count, tile_vals):
    span, width = features.shape
    n_z4, n_z1, n_core = lax.axis_size(Z4), lax.axis_size("z1"), lax.axis_size("core")
    n_y, n_zh, n_x = lax.axis_size("y"), lax.axis_size("zh"), lax.axis_size("x")
    n_line = n_z4 * n_z1
    n_row, n_col = n_line * n_core, n_y * n_zh * n_x
    n_plane = n_y * n_x
    my_row = lax.axis_index(ROW)
    my_zh = lax.axis_index("zh")
    slots = tile_vals.shape[2]
    nodes = n_row * n_col * span
    tiles = tile_vals[0, 0]
    count = tile_count[0]
    row_index = tile_rows[0, 0]
    col_index = tile_cols[0, 0]
    col_bits = col_index ^ my_row
    col_place = (col_bits & 1) * n_line + (col_bits & 2) * (n_z4 // 2)
    col_place = col_place + ((col_bits >> 2) & 1) * 2 + (col_bits >> 3)
    row_plane = (row_index >> 3) * n_x + (row_index & 3)
    row_place = (((row_index >> 2) & 1) ^ my_zh) * n_plane + row_plane

    alive = (jnp.arange(slots, dtype=jnp.int32) < count[0]).astype(F32)
    order_cols = (col_index[:, None] == jnp.arange(n_row, dtype=jnp.int32)[None, :]).astype(F32)
    col_sums = jnp.sum(tiles, axis=1, dtype=F32) * alive[:, None]
    degree_terms = jnp.einsum("sc,sj->cj", order_cols, col_sums, precision=lax.Precision.HIGHEST)
    high = lax.reduce_precision(degree_terms, 8, 7)
    pieces = jnp.stack([high, degree_terms - high]).astype(BF16)
    chunk = width // CHUNKS
    parts = [slice(c * chunk, (c + 1) * chunk) for c in range(CHUNKS)]
    held = [features[None, :, part] for part in parts]
    held[0] = jnp.concatenate([held[0], pieces.reshape(1, -1, chunk)], axis=1)
    for axis in Z4:
        held = [jnp.concatenate([part, flip(part, axis)]) for part in held]
    pairs = [flip(part, "z1") for part in held]
    groups = [held, pairs] + [[flip(part, "core") for part in group] for group in (held, pairs)]

    def degrees(part):
        return jnp.sum(part[:, span:].astype(F32).reshape(-1, n_row, span), axis=0)

    col_scale = lax.rsqrt(1.0 + sum(degrees(group[0]) for group in groups))
    own_scale = lax.dynamic_index_in_dim(col_scale, my_row, axis=0, keepdims=False)
    slot_scale = col_scale[col_index]

    near_terms, far_terms = tile_sums(
        False,
        col_place,
        row_place,
        count,
        tiles,
        slot_scale,
        sum(groups, []),
        [[[(g * CHUNKS + c, 0, span)] for c in range(CHUNKS)] for g in range(len(groups))],
        [(0, width, 0, n_plane), (0, width, n_plane, n_col)],
    )
    far_sum = jnp.sum(swap_parts(far_terms, PLANE).astype(F32), axis=0).astype(BF16)
    near_group = swap_parts(after(near_terms, far_sum), PLANE)
    own_total = jnp.sum(near_group.astype(F32), axis=0) + flip(far_sum, "zh").astype(F32)

    output, normed, grad_pre, grad_own = layer_rows(own_total, cotangent, weight)

    lead = span * 3 // 8
    weight_terms = jnp.einsum("nf,ng->fg", normed, grad_pre, preferred_element_type=F32)
    weight_parts = weight_terms.astype(BF16).reshape(n_plane, width // n_plane, width)
    first_group = swap_parts(
        jnp.concatenate([copies_of(grad_own[:lead], PLANE), weight_parts], axis=1), PLANE
    )
    grad_rest = jnp.concatenate([grad_own[lead:], flip(grad_own, "zh")])
    last_group = swap_parts(copies_of(after(grad_rest, first_group), PLANE), PLANE)

    line_rows = jnp.sum(first_group[:, lead:].astype(F32), axis=0)
    for axis in ("core", "zh", "z1", "zb", "za"):
        line_rows = line_rows + flip(line_rows, axis)
    line_rows = line_rows * (1.0 / math.sqrt(nodes))
    last_group = after(last_group, line_rows)

    halves = tile_sums(
        True,
        row_place,
        col_place,
        count,
        tiles,
        None,
        [first_group, last_group],
        [[[(0, 0, lead), (1, 0, span - lead)]], [[(1, span - lead, 2 * span - lead)]]],
        [(part.start, part.stop, first, first + n_line) for first in (0, n_line) for part in parts],
    )
    totals = [
        keep.astype(F32) + flip(send, "core").astype(F32)
        for keep, send in zip(halves[:CHUNKS], halves[CHUNKS:])
    ]
    along = jnp.concatenate([total[0, :8] for total in totals], axis=1)
    weight_rows = swap_parts(copies_of(jnp.concatenate([line_rows, along]), PLANE), PLANE)
    weight_grad = weight_rows[:, : line_rows.shape[0]].reshape(width, width)
    for axis in ("z1", "zb", "za"):
        totals = [total.astype(BF16) for total in totals]
        size = totals[0].shape[0] // 2
        totals = [
            total[:size].astype(F32) + flip(total[size:], axis).astype(F32) for total in totals
        ]
    feature_grad = jnp.concatenate([total[0] for total in totals], axis=1) * own_scale[:, None]
    return (output, weight_grad, feature_grad)


def solution(mesh):
    fine = Mesh(mesh.devices.reshape(2, 2, 2, 2, 4, 2, 4), AXES)
    nodes, row, col = P(AXES, None), ROW, ("y", "zh", "x")
    in_specs = (
        nodes,
        P(),
        nodes,
        P(row, col, None),
        P(row, col, None),
        P(row, col),
        P(row, col, None, None, None),
    )
    out_specs = (nodes, P(), nodes)
    return jax.shard_map(local, mesh=fine, in_specs=in_specs, out_specs=out_specs, check_vma=False)
```

```python
import functools
import math

import jax
import jax.numpy as jnp
from jax import lax
from jax.experimental import pallas as pl
from jax.experimental.pallas import tpu as pltpu
from jax.sharding import Mesh
from jax.sharding import PartitionSpec as P

AXES = ("za", "zb", "z1", "core", "y", "zh", "x")
Z4 = ("za", "zb")
ROW = ("za", "zb", "z1", "core")
PLANE = ("y", "x")
CHUNKS = 2
BF16 = jnp.bfloat16
F32 = jnp.float32


def layer_rows(row_total, grad_rows, weight):
    inv_rms = lax.rsqrt(jnp.mean(row_total * row_total, axis=1, keepdims=True) + 1e-06)
    norm_f32 = row_total * inv_rms
    normed = norm_f32.astype(BF16)
    pre_act = jnp.dot(normed, weight, preferred_element_type=F32)
    output = jax.nn.silu(pre_act).astype(BF16)
    sigmoid_pre = jax.nn.sigmoid(pre_act)
    act_slope = sigmoid_pre * (1.0 + pre_act * (1.0 - sigmoid_pre))
    grad_pre = (grad_rows.astype(F32) * act_slope).astype(BF16)
    grad_norm = jnp.einsum("ng,fg->nf", grad_pre, weight, preferred_element_type=F32)
    grad_z = (
        inv_rms * (grad_norm - norm_f32 * jnp.mean(grad_norm * norm_f32, axis=1, keepdims=True))
    ).astype(BF16)
    return (output, normed, grad_pre, grad_z)


def flip(block, axis):
    return lax.ppermute(block, axis, [(0, 1), (1, 0)])


def after(value, *others):
    return lax.optimization_barrier((value,) + others)[0]


def swap_parts(parts, axes):
    return lax.all_to_all(parts, axes, split_axis=0, concat_axis=0, tiled=True)


def copies_of(block, axes):
    return jnp.broadcast_to(block[None], (lax.axis_size(axes),) + block.shape)


def tile_kernel(transposed, scaled, sources, places, source, target, count, tiles, *refs):
    scale, refs = (refs[0], refs[1:]) if scaled else (None, refs)
    total = refs[-1]
    arrays, outputs = refs[: -1 - len(places)], refs[-1 - len(places) : -1]
    slots, size, _ = tiles.shape
    axis = 0 if transposed else 1
    for output in outputs:
        output[...] = jnp.zeros_like(output)
    total[...] = jnp.zeros_like(total)
    owners = []
    for slot in range(slots):
        owner = jnp.int32(slot)
        for earlier in reversed(range(slot)):
            owner = jnp.where(target[earlier] == target[slot], earlier, owner)
        owners.append(owner)

    for slot in range(slots):

        def add(block, left):
            if scaled:
                row = jnp.broadcast_to(scale[slot : slot + 1, :], (size, size))
                column = jnp.transpose(row)
                lanes = [block[:, i : i + size] for i in range(0, block.shape[1], size)]
                lanes = [(part.astype(F32) * column).astype(BF16) for part in lanes]
                block = jnp.concatenate(lanes, axis=1)
            total[owners[slot], :, left : left + block.shape[1]] += lax.dot_general(
                tiles[slot], block, (((axis,), (0,)), ((), ())), preferred_element_type=F32
            )

        first = 0
        for chunks in sources:
            held = arrays[chunks[0][0][0]].shape[0]
            inside = source[slot] - first
            first += held

            @pl.when((slot < count[0]) & (inside >= 0) & (inside < held))
            def _(chunks=chunks, inside=jnp.clip(inside, 0, held - 1)):
                left = 0
                for pieces in chunks:
                    rows = [arrays[number][inside, low:high, :] for number, low, high in pieces]
                    block = rows[0] if len(rows) == 1 else jnp.concatenate(rows, axis=0)
                    add(block, left)
                    left += block.shape[1]

    for slot in range(slots):
        for output, (left, right, start, stop) in zip(outputs, places):
            place = target[slot] - start
            held = (place >= 0) & (place < stop - start)

            @pl.when((slot < count[0]) & (owners[slot] == slot) & held)
            def _(output=output, left=left, right=right, place=jnp.clip(place, 0, stop - start - 1)):
                output[place] = total[slot, :, left:right].astype(BF16)


def tile_sums(transposed, source, target, count, tiles, scale, arrays, sources, places):
    slots, size, _ = tiles.shape
    width = sum(arrays[pieces[0][0]].shape[2] for pieces in sources[0])
    smem = pl.BlockSpec(memory_space=pltpu.SMEM)
    vmem = pl.BlockSpec(memory_space=pltpu.VMEM)
    scaled = scale is not None
    operands = [tiles] + [scale] * scaled + list(arrays)
    shapes = [(stop - start, size, right - left) for left, right, start, stop in places]
    moved = sum(math.prod(shape) for shape in shapes) + sum(array.size for array in arrays)
    return pl.pallas_call(
        functools.partial(tile_kernel, transposed, scaled, sources, places),
        out_shape=[jax.ShapeDtypeStruct(shape, BF16) for shape in shapes],
        in_specs=[smem] * 3 + [vmem] * len(operands),
        out_specs=[vmem] * len(shapes),
        scratch_shapes=[pltpu.VMEM((slots, size, width), F32)],
        compiler_params=pltpu.CompilerParams(vmem_limit_bytes=40 * 1024 * 1024),
        cost_estimate=pl.CostEstimate(
            flops=2 * slots * size * size * width,
            bytes_accessed=2 * moved,
            transcendentals=0,
        ),
    )(source, target, count, *operands)


def local(features, weight, cotangent, tile_rows, tile_cols, tile_count, tile_vals):
    span, width = features.shape
    n_z4, n_z1, n_core = lax.axis_size(Z4), lax.axis_size("z1"), lax.axis_size("core")
    n_y, n_zh, n_x = lax.axis_size("y"), lax.axis_size("zh"), lax.axis_size("x")
    n_line = n_z4 * n_z1
    n_row, n_col = n_line * n_core, n_y * n_zh * n_x
    n_plane = n_y * n_x
    my_row = lax.axis_index(ROW)
    my_zh = lax.axis_index("zh")
    slots = tile_vals.shape[2]
    nodes = n_row * n_col * span
    tiles = tile_vals[0, 0]
    count = tile_count[0]
    row_index = tile_rows[0, 0]
    col_index = tile_cols[0, 0]
    col_bits = col_index ^ my_row
    col_place = (col_bits & 1) * n_line + (col_bits & 2) * (n_z4 // 2)
    col_place = col_place + ((col_bits >> 2) & 1) * 2 + (col_bits >> 3)
    row_plane = (row_index >> 3) * n_x + (row_index & 3)
    row_place = (((row_index >> 2) & 1) ^ my_zh) * n_plane + row_plane

    alive = (jnp.arange(slots, dtype=jnp.int32) < count[0]).astype(F32)
    order_cols = (col_index[:, None] == jnp.arange(n_row, dtype=jnp.int32)[None, :]).astype(F32)
    col_sums = jnp.sum(tiles, axis=1, dtype=F32) * alive[:, None]
    degree_terms = jnp.einsum("sc,sj->cj", order_cols, col_sums, precision=lax.Precision.HIGHEST)
    high = lax.reduce_precision(degree_terms, 8, 7)
    pieces = jnp.stack([high, degree_terms - high]).astype(BF16)
    chunk = width // CHUNKS
    parts = [slice(c * chunk, (c + 1) * chunk) for c in range(CHUNKS)]
    held = [features[None, :, part] for part in parts]
    held[0] = jnp.concatenate([held[0], pieces.reshape(1, -1, chunk)], axis=1)
    for axis in Z4:
        held = [jnp.concatenate([part, flip(part, axis)]) for part in held]
    pairs = [flip(part, "z1") for part in held]
    groups = [held, pairs] + [[flip(part, "core") for part in group] for group in (held, pairs)]

    def degrees(part):
        return jnp.sum(part[:, span:].astype(F32).reshape(-1, n_row, span), axis=0)

    col_scale = lax.rsqrt(1.0 + sum(degrees(group[0]) for group in groups))
    own_scale = lax.dynamic_index_in_dim(col_scale, my_row, axis=0, keepdims=False)
    slot_scale = col_scale[col_index]

    near_terms, far_terms = tile_sums(
        False,
        col_place,
        row_place,
        count,
        tiles,
        slot_scale,
        sum(groups, []),
        [[[(g * CHUNKS + c, 0, span)] for c in range(CHUNKS)] for g in range(len(groups))],
        [(0, width, 0, n_plane), (0, width, n_plane, n_col)],
    )
    far_sum = jnp.sum(swap_parts(far_terms, PLANE).astype(F32), axis=0).astype(BF16)
    near_group = swap_parts(after(near_terms, far_sum), PLANE)
    own_total = jnp.sum(near_group.astype(F32), axis=0) + flip(far_sum, "zh").astype(F32)

    output, normed, grad_pre, grad_own = layer_rows(own_total, cotangent, weight)

    lead = span * 3 // 8
    weight_terms = jnp.einsum("nf,ng->fg", normed, grad_pre, preferred_element_type=F32)
    weight_parts = weight_terms.astype(BF16).reshape(n_plane, width // n_plane, width)
    first_group = swap_parts(
        jnp.concatenate([copies_of(grad_own[:lead], PLANE), weight_parts], axis=1), PLANE
    )
    grad_rest = jnp.concatenate([grad_own[lead:], flip(grad_own, "zh")])
    last_group = swap_parts(copies_of(after(grad_rest, first_group), PLANE), PLANE)

    line_rows = jnp.sum(first_group[:, lead:].astype(F32), axis=0)
    for axis in ("core", "z1", "za", "zb", "zh"):
        line_rows = line_rows + flip(line_rows, axis)
    line_rows = line_rows * (1.0 / math.sqrt(nodes))
    last_group = after(last_group, line_rows)

    halves = tile_sums(
        True,
        row_place,
        col_place,
        count,
        tiles,
        None,
        [first_group, last_group],
        [[[(0, 0, lead), (1, 0, span - lead)]], [[(1, span - lead, 2 * span - lead)]]],
        [(part.start, part.stop, first, first + n_line) for first in (0, n_line) for part in parts],
    )
    totals = [
        keep.astype(F32) + flip(send, "core").astype(F32)
        for keep, send in zip(halves[:CHUNKS], halves[CHUNKS:])
    ]
    along = jnp.concatenate([total[0, :8] for total in totals], axis=1)
    weight_rows = swap_parts(copies_of(jnp.concatenate([line_rows, along]), PLANE), PLANE)
    weight_grad = weight_rows[:, : line_rows.shape[0]].reshape(width, width)
    for axis in ("z1", "zb", "za"):
        totals = [total.astype(BF16) for total in totals]
        size = totals[0].shape[0] // 2
        totals = [
            total[:size].astype(F32) + flip(total[size:], axis).astype(F32) for total in totals
        ]
    feature_grad = jnp.concatenate([total[0] for total in totals], axis=1) * own_scale[:, None]
    return (output, weight_grad, feature_grad)


def solution(mesh):
    fine = Mesh(mesh.devices.reshape(2, 2, 2, 2, 4, 2, 4), AXES)
    nodes, row, col = P(AXES, None), ROW, ("y", "zh", "x")
    in_specs = (
        nodes,
        P(),
        nodes,
        P(row, col, None),
        P(row, col, None),
        P(row, col),
        P(row, col, None, None, None),
    )
    out_specs = (nodes, P(), nodes)
    return jax.shard_map(local, mesh=fine, in_specs=in_specs, out_specs=out_specs, check_vma=False)
```
